32 devices in a mesh: groups: 2 (over y), tile: 4 (over x, core), cuts: 4 (over z).
Axes of the slice: x: 2, y: 2, z: 4, core: 2. Of those that a mesh axis runs over, the one named last changes fastest.
Arguments:
- trade: bfloat16 [16, 4, 256, 8192], P(('groups', 'cuts'), 'tile'), parts along dimension 0, may hold values from -6 to 6
- factor: bfloat16 [32768, 256], P(('groups', 'tile', 'cuts')), parts along dimension 0, may hold values from -0.375 to 0.375
- scales: float32 [16, 256], P(('groups', 'cuts')), parts along dimension 0, may hold values from 0.1 to 1.9
- core: float32 [512, 256], P('groups'), parts along dimension 0, may hold values from -4 to 4
Outputs:
- grad_factor: float32 [32768, 256], P(('groups', 'tile', 'cuts')), parts along dimension 0
- grad_window: float32 [1024, 256], P(('groups', 'cuts')), parts along dimension 0
- grad_core: float32 [512, 256], P('groups'), parts along dimension 0
- grad_scales: float32 [16, 256], P(('groups', 'cuts')), parts along dimension 0
The draws below stay inside these ranges and needn't reach their ends.
There are 2 independent parts, one for each index of `groups`. The reference program is written for one: setup_inputs(seed, part) draws one part's arguments, and reference() takes and returns one part's arrays. A program takes and returns all parts, laid end to end along the dimension named above; each array names one. Nothing has to cross between parts.
All inputs are finite; a program needn't handle non-finite values.
Results may differ from the reference program's by a relative error of at most 0.00055.
Values may be sent and summed in bfloat16 or wider, within the bound.
No kernel may reach another device: no remote copies, remote signals or barrier semaphores. Data moves between devices by JAX's collectives and lax.ppermute only.
A program may use at most 128 MiB of HBM per device.

```python
import math
import jax
import jax.numpy as jnp
from jax import lax

N = 16384
P_SIZE = 256
TR = 2
ROWS_DEV = 256
K = 8
W = 512
COLS_DEV = 8192
N_TILE = 4


def with_spikes(drawn, key, source, target, parts, factor):
    def block_of(axis_at):
        return (jnp.arange(drawn.shape[axis_at]) // (drawn.shape[axis_at] // parts)).reshape((-1,) + (1,) * (drawn.ndim - 1 - axis_at))

    one_side = jax.random.permutation(key, parts)[block_of(target)]
    other_side = (block_of(target) + parts // 2) % parts
    return jnp.where((block_of(source) == one_side) | (block_of(source) == other_side), factor * drawn, drawn)


def shard_levels(rng, extent, cuts, low, high):
    gain = 1.0
    for dim, shards_of in cuts:
        steps = jax.random.uniform(jax.random.fold_in(jax.random.fold_in(rng, 6), dim), (shards_of,), jnp.float32, low / len(cuts), high / len(cuts))
        gain = gain * jnp.repeat(jnp.exp(steps), extent[dim] // shards_of).reshape((-1,) + (1,) * (len(extent) - 1 - dim))
    return gain


def noise(rng, dims, scale, bound, shards=(), held_as=jnp.bfloat16):
    entries = jax.random.normal(rng, dims, jnp.float32) * scale
    if len(shards) > 0:
        entries = shard_levels(rng, dims, shards, -0.22, 0.18) * entries
    return jnp.clip(entries, min=-bound, max=bound).astype(held_as)


def gaussian_with(own_key, extent, spread, limit, split, heavy, held_as=jnp.bfloat16):
    values = spread * jax.random.normal(own_key, extent, jnp.float32)
    if split:
        values = values * shard_levels(own_key, extent, split, -0.22, 0.18)
    return jnp.clip(with_spikes(values, jax.random.fold_in(own_key, 3), *heavy), -limit, limit).astype(held_as)


def setup_inputs(seed: int = 0, part: int = 0) -> dict:
    arg_keys = jax.random.split(jax.random.key(seed), 5)
    part_keys = jax.random.split(jax.random.fold_in(arg_keys[4], part), 5)
    return {
        "trade": gaussian_with(part_keys[0], (K, N_TILE, ROWS_DEV, COLS_DEV), 1.0, 6.0, ((0, 4), (1, 4)), (0, 3, 4, 2.0)),
        "factor": noise(part_keys[1], (N, P_SIZE), P_SIZE ** -0.5, 0.375, ((0, 16),)),
        "scales": jnp.clip(1.0 + 0.18 * jax.random.normal(part_keys[2], (K, P_SIZE), jnp.float32), 0.1, 1.9),
        "core": noise(part_keys[3], (P_SIZE, P_SIZE), 1.0, 4.0, (), jnp.float32),
    }


def reference(trade, factor, scales, core):
    bands = N_TILE // TR
    rows_band = ROWS_DEV
    cols_band = N // bands
    window32 = factor[:W].astype(jnp.float32)
    coef = 1.0 / math.sqrt(K * W)
    highest = lax.Precision.HIGHEST

    def one_month(carry, inputs):
        acc_factor, acc_window, acc_core = carry
        tiles, diag_k = inputs
        matrix = tiles.reshape(bands, TR, rows_band, cols_band).transpose(1, 2, 0, 3).reshape(W, N)
        inner = diag_k[:, None] * core * diag_k[None, :]
        mapped = jnp.dot(window32, inner, precision=highest).astype(jnp.bfloat16)
        model = jnp.dot(mapped, factor.T, preferred_element_type=jnp.float32)
        residual = (matrix.astype(jnp.float32) - model).astype(jnp.bfloat16)
        acc_factor = acc_factor + jnp.dot(residual.T, mapped, preferred_element_type=jnp.float32)
        projected = jnp.dot(residual, factor, preferred_element_type=jnp.float32)
        acc_window = acc_window + jnp.dot(projected, inner.T, precision=highest)
        gram = jnp.dot(window32.T, projected, precision=highest)
        acc_core = acc_core + diag_k[:, None] * gram * diag_k[None, :]
        weighted = gram * core
        grad_diag = jnp.dot(weighted, diag_k, precision=highest) + jnp.dot(weighted.T, diag_k, precision=highest)
        return ((acc_factor, acc_window, acc_core), grad_diag)
    start = (jnp.zeros((N, P_SIZE), jnp.float32), jnp.zeros((W, P_SIZE), jnp.float32), jnp.zeros((P_SIZE, P_SIZE), jnp.float32))
    (acc_factor, acc_window, acc_core), grad_diags = lax.scan(one_month, start, (trade, scales))
    return (-coef * acc_factor, -coef * acc_window, -coef * acc_core, -coef * grad_diags)
```

```python
import functools
import math

import jax
import jax.numpy as jnp
from jax import lax
from jax.experimental import pallas as pl
from jax.experimental.pallas import tpu as pltpu
from jax.sharding import PartitionSpec as P

P_SIZE = 256
F32, BF16, F16 = jnp.float32, jnp.bfloat16, jnp.float16
NN = (((1,), (0,)), ((), ()))
NT = (((1,), (1,)), ((), ()))
TN = (((0,), (0,)), ((), ()))
VMEM_LIMIT = 48 * 2**20


def dot(a, b, dims, **more):
    return lax.dot_general(a, b, dims, preferred_element_type=F32, **more)


def split3(value):
    first = value.astype(BF16)
    rest = value - first.astype(F32)
    second = rest.astype(BF16)
    return first, second, (rest - second.astype(F32)).astype(BF16)


def swapped(value, axis, mask):
    pairs = [(source, source ^ mask) for source in range(lax.axis_size(axis))]
    return lax.ppermute(value, axis, pairs)


def mapped_kernel(core_ref, window_ref, inner_ref, mapped_ref, turned_ref):
    rows = window_ref.shape[0] // 2
    at = core_ref[0]
    own = window_ref[pl.ds(pl.multiple_of(at * rows, rows), rows), :]
    other = window_ref[pl.ds(pl.multiple_of((1 - at) * rows, rows), rows), :]
    window = jnp.concatenate([own, other], 0)
    for month in range(inner_ref.shape[0]):
        value = sum(dot(window, term, NN) for term in split3(inner_ref[month]))
        rounded = value.astype(BF16)
        mapped_ref[month] = rounded
        turned_ref[:, month * 2 * rows : (month + 1) * 2 * rows] = rounded.astype(F32).T.astype(BF16)


def mapped_call(core_at, window, inner):
    months, size = inner.shape[0], window.shape[0]
    return pl.pallas_call(
        mapped_kernel,
        out_shape=[
            jax.ShapeDtypeStruct((months, size, P_SIZE), BF16),
            jax.ShapeDtypeStruct((P_SIZE, months * size), BF16),
        ],
        in_specs=[
            pl.BlockSpec(memory_space=pltpu.SMEM),
            pl.BlockSpec(memory_space=pltpu.VMEM),
            pl.BlockSpec(memory_space=pltpu.VMEM),
        ],
        out_specs=[pl.BlockSpec(memory_space=pltpu.VMEM)] * 2,
        compiler_params=pltpu.CompilerParams(vmem_limit_bytes=VMEM_LIMIT),
        cost_estimate=pl.CostEstimate(
            flops=6 * months * size * P_SIZE * P_SIZE, bytes_accessed=2 * 2**20, transcendentals=0
        ),
        name="mapped",
    )(core_at, window, inner)


def encoded(value):
    peak = jnp.max(jnp.abs(value), axis=0, keepdims=True)
    exponent = jnp.ceil(jnp.log2(jnp.maximum(peak, 1e-30)))
    return value * jnp.exp2(15.0 - exponent), jnp.broadcast_to(exponent, (16, value.shape[1]))


def piece_kernel(scaled, at_ref, own_ref, other_ref, block_ref, mapped_ref, turned_ref, grad_ref, proj_ref):
    step = pl.program_id(0)
    block = block_ref[...]
    months, size = mapped_ref.shape[0], mapped_ref.shape[1]
    rows = size // 2
    model = dot(mapped_ref[...].reshape(months * size, P_SIZE), block, NT)
    parts = []
    for month in range(months):
        for band in range(2):
            flows = own_ref[month, 0] if band == 0 else other_ref[month]
            at = (2 * month + band) * rows
            parts.append((flows.astype(F32) - model[at : at + rows]).astype(BF16))
    residual = jnp.concatenate(parts, 0)
    grad = dot(turned_ref[...], residual, NN)
    if scaled:
        value, exponent = encoded(grad)
        grad_ref[:P_SIZE, :] = value
        grad_ref[P_SIZE:, :] = exponent
    else:
        grad_ref[...] = grad
    projected = dot(residual, block, NN).reshape(proj_ref.shape)

    @pl.when(step == 0)
    def _():
        proj_ref[...] = projected

    @pl.when(step > 0)
    def _():
        proj_ref[...] += projected


def piece_call(at, trade, other, block, mapped, turned, scaled, label):
    months, size = mapped.shape[0], mapped.shape[1]
    rows, columns = size // 2, block.shape[0]
    width = min(512, columns)
    steps = columns // width
    high = P_SIZE + 16 if scaled else P_SIZE
    spec = pltpu.PrefetchScalarGridSpec(
        num_scalar_prefetch=1,
        grid=(steps,),
        in_specs=[
            pl.BlockSpec((months, 1, rows, width), lambda j, s: (0, 0, 0, s[0] * steps + j)),
            pl.BlockSpec((months, rows, width), lambda j, s: (0, 0, s[1] * steps + j)),
            pl.BlockSpec((width, P_SIZE), lambda j, s: (j, 0)),
            pl.BlockSpec((months, size, P_SIZE), lambda j, s: (0, 0, 0)),
            pl.BlockSpec((P_SIZE, months * size), lambda j, s: (0, 0)),
        ],
        out_specs=[
            pl.BlockSpec((high, width), lambda j, s: (0, j)),
            pl.BlockSpec((months, size, P_SIZE), lambda j, s: (0, 0, 0)),
        ],
    )
    return pl.pallas_call(
        functools.partial(piece_kernel, scaled),
        grid_spec=spec,
        out_shape=[
            jax.ShapeDtypeStruct((high, columns), F32),
            jax.ShapeDtypeStruct((months, size, P_SIZE), F32),
        ],
        compiler_params=pltpu.CompilerParams(vmem_limit_bytes=VMEM_LIMIT),
        cost_estimate=pl.CostEstimate(
            flops=6 * months * size * columns * P_SIZE,
            bytes_accessed=2 * months * size * columns + 4 * 2**20,
            transcendentals=0,
        ),
        name=label,
    )(at, trade, other, block, mapped, turned)


def relay_kernel(first_ref, second_ref, out_ref):
    received = first_ref[:P_SIZE, :] * jnp.exp2(first_ref[P_SIZE : P_SIZE + 1, :] - 15.0)
    value, exponent = encoded(received + second_ref[...])
    out_ref[:P_SIZE, :] = value
    out_ref[P_SIZE:, :] = exponent


def relay_call(received, own):
    columns = own.shape[1]
    width = columns // 2
    return pl.pallas_call(
        relay_kernel,
        grid=(2,),
        in_specs=[
            pl.BlockSpec((P_SIZE + 16, width), lambda j: (0, j)),
            pl.BlockSpec((P_SIZE, width), lambda j: (0, j)),
        ],
        out_specs=pl.BlockSpec((P_SIZE + 16, width), lambda j: (0, j)),
        out_shape=jax.ShapeDtypeStruct((P_SIZE + 16, columns), F32),
        compiler_params=pltpu.CompilerParams(vmem_limit_bytes=VMEM_LIMIT),
        cost_estimate=pl.CostEstimate(flops=10 * P_SIZE * columns, bytes_accessed=3 * 2**20, transcendentals=0),
        name="relay",
    )(received, own)


def final_kernel(coef, own_ref, near_ref, far_ref, out_ref):
    total = own_ref[...]
    for ref in (near_ref, far_ref):
        total = total + ref[:P_SIZE, :] * jnp.exp2(ref[P_SIZE : P_SIZE + 1, :] - 15.0)
    out_ref[...] = (-coef * total).T


def final_call(coef, own, near, far):
    columns = own.shape[1]
    width = columns // 2
    tall = pl.BlockSpec((P_SIZE + 16, width), lambda j: (0, j))
    return pl.pallas_call(
        functools.partial(final_kernel, coef),
        grid=(2,),
        in_specs=[pl.BlockSpec((P_SIZE, width), lambda j: (0, j)), tall, tall],
        out_specs=pl.BlockSpec((width, P_SIZE), lambda j: (j, 0)),
        out_shape=jax.ShapeDtypeStruct((columns, P_SIZE), F32),
        compiler_params=pltpu.CompilerParams(vmem_limit_bytes=VMEM_LIMIT),
        cost_estimate=pl.CostEstimate(flops=10 * P_SIZE * columns, bytes_accessed=4 * 2**20, transcendentals=0),
        name="final",
    )(own, near, far)


def terms_kernel(cuts, at_ref, window_ref, inner_ref, core_ref, scales_ref, columns_ref, *rest):
    projs, (keep_ref, send_ref, acc_ref) = rest[:-3], rest[-3:]
    months, size = projs[0].shape[0], projs[0].shape[1]
    rows = size // 2
    at = at_ref[0]
    own = window_ref[pl.ds(pl.multiple_of(at * rows, rows), rows), :]
    other = window_ref[pl.ds(pl.multiple_of((1 - at) * rows, rows), rows), :]
    window = jnp.concatenate([own, other], 0)
    core = core_ref[...]
    acc_window = jnp.zeros((size, P_SIZE), F32)
    acc_core = jnp.zeros((P_SIZE, P_SIZE), F32)
    diagonals = []
    for month in range(months):
        proj = projs[0][month]
        for ref in projs[1:]:
            proj = proj + ref[month]
        acc_window = acc_window + dot(proj, inner_ref[month], NT, precision=lax.Precision.HIGHEST)
        gram = sum(dot(window, term, TN) for term in split3(proj))
        down = columns_ref[:, month : month + 1]
        acc_core = acc_core + down * gram * scales_ref[month : month + 1, :]
        weighted = gram * core
        diagonals.append(jnp.sum((weighted + weighted.T) * down, axis=0, keepdims=True))
    diagonals.append(jnp.zeros((8 - months, P_SIZE), F32))
    diagonal = jnp.concatenate(diagonals, 0)
    acc_ref[pl.ds(pl.multiple_of(at * rows, rows), rows), :] = acc_window[:rows]
    acc_ref[pl.ds(pl.multiple_of((1 - at) * rows, rows), rows), :] = acc_window[rows:]
    acc_ref[size:, :] = acc_core
    w = size // (4 * cuts)
    q = P_SIZE // 4
    half = cuts * w + q
    for ref, which in ((keep_ref, at), (send_ref, 1 - at)):
        for x in range(2):
            for cut in range(cuts):
                start = pl.multiple_of(cut * 4 * w + which * 2 * w + x * w, 8)
                ref[x * half + cut * w : x * half + (cut + 1) * w, :] = acc_ref[pl.ds(start, w), :]
            start = pl.multiple_of(size + which * 2 * q + x * q, 8)
            ref[x * half + cuts * w : (x + 1) * half, :] = acc_ref[pl.ds(start, q), :]
        ref[2 * half :, :] = diagonal


def terms_call(cuts, core_at, window, inner, core, scales, projs):
    months, size = projs[0].shape[0], projs[0].shape[1]
    high = size // 2 + P_SIZE // 2 + 8
    vmem = pl.BlockSpec(memory_space=pltpu.VMEM)
    return pl.pallas_call(
        functools.partial(terms_kernel, cuts),
        in_specs=[pl.BlockSpec(memory_space=pltpu.SMEM)] + [vmem] * (5 + len(projs)),
        out_specs=[vmem, vmem],
        out_shape=[jax.ShapeDtypeStruct((high, P_SIZE), F32)] * 2,
        scratch_shapes=[pltpu.VMEM((size + P_SIZE, P_SIZE), F32)],
        compiler_params=pltpu.CompilerParams(vmem_limit_bytes=VMEM_LIMIT),
        cost_estimate=pl.CostEstimate(
            flops=18 * months * size * P_SIZE * P_SIZE, bytes_accessed=6 * 2**20, transcendentals=0
        ),
        name="terms",
    )(core_at, window, inner, core, scales, scales.T, *projs)


def body_line(trade, factor, scales, core):
    cuts = lax.axis_size("cuts")
    tile, cut = lax.axis_index("tile"), lax.axis_index("cuts")
    x, at = tile // 2, tile % 2
    months, rows = trade.shape[0], trade.shape[2]
    size, piece = 2 * rows, factor.shape[0]
    coef = 1.0 / math.sqrt(months * cuts * size)
    core_at = at.astype(jnp.int32).reshape(1)
    inner = scales[:, :, None] * core[None] * scales[:, None, :]

    head = factor[:size]
    sent = [lax.ppermute(head, ("tile", "cuts"), [(0, target)]) for target in range(1, cuts)]
    line = jnp.where(cut == 0, head, sum(sent[1:], sent[0]))
    across = lax.ppermute(line, "tile", [(0, 2)])
    even = jnp.where(x == 0, line, across)
    window = jnp.where(at == 0, even, lax.ppermute(even, "tile", [(0, 1), (2, 3)]))

    near = swapped(factor, "cuts", 1)
    middle = swapped(factor, "cuts", 2)
    far = swapped(middle, "cuts", 1)

    half = cuts * piece
    give = lax.dynamic_slice_in_dim(trade[:, 0], (1 - at) * half, half, 2)
    other = swapped(give, "tile", 1)

    mapped, turned = mapped_call(core_at, window, inner)

    def piece_of(which, block, scaled, label):
        where = jnp.stack([at * cuts + which, which]).astype(jnp.int32)
        return piece_call(where, trade, other, block, mapped, turned, scaled, label)

    grad_near, proj_near = piece_of(cut ^ 1, near, True, "piece_near")
    from_near = swapped(grad_near.astype(F16), "cuts", 1)
    grad_own, proj_own = piece_of(cut, factor, False, "piece_own")
    grad_middle, proj_middle = piece_of(cut ^ 2, middle, False, "piece_middle")
    grad_far, proj_far = piece_of(cut ^ 3, far, True, "piece_far")
    joined = swapped(grad_far.astype(F16), "cuts", 1)

    keep, send = terms_call(cuts, core_at, window, inner, core, scales, [proj_near, proj_own, proj_middle, proj_far])
    both = keep + swapped(send, "tile", 1)
    w, q = size // (4 * cuts), P_SIZE // 4
    part = cuts * w + q
    low, high, diagonal = both[:part], both[part : 2 * part], both[2 * part :]
    keep = jnp.concatenate([jnp.where(x == 0, low, high), diagonal], 0)
    send = jnp.concatenate([jnp.where(x == 0, high, low), diagonal], 0)
    quarter = keep + swapped(send, "tile", 2)
    diagonal = quarter[part : part + months]
    core_part = quarter[cuts * w : part]

    def for_cut(which):
        return jnp.concatenate([lax.dynamic_slice_in_dim(quarter, which * w, w, 0), core_part], 0)

    total = for_cut(cut)
    for mask in range(1, cuts):
        total = total + swapped(for_cut(cut ^ mask), "cuts", mask)

    def joined_pair(mine, theirs, first):
        return jnp.where(first, mine, theirs), jnp.where(first, theirs, mine)

    first, second = joined_pair(total, swapped(total, "tile", 2), x == 0)
    line_total = jnp.concatenate([first[:w], second[:w], first[w:], second[w:]], 0)
    first, second = joined_pair(line_total, swapped(line_total, "tile", 1), at == 0)
    grad_window = jnp.concatenate([first[: 2 * w], second[: 2 * w]], 0)
    grad_core = jnp.concatenate([first[2 * w :], second[2 * w :]], 0)

    passed = relay_call(joined.astype(F32), grad_middle)
    from_far = swapped(passed.astype(F16), "cuts", 2)
    grad_factor = final_call(coef, grad_own, from_near.astype(F32), from_far.astype(F32))
    return (grad_factor, -coef * grad_window, -coef * grad_core, -coef * diagonal)


def from_root(block, axis, source):
    block = jnp.where(lax.axis_index(axis) == source, block, jnp.zeros_like(block))
    return lax.psum(block, axis)


def body_any(trade, factor, scales, core):
    n_cuts = lax.axis_size("cuts")
    band_index = lax.axis_index("tile") % 2
    months = trade.shape[0]
    rows_band = trade.shape[2]
    window_size = 2 * rows_band
    highest = lax.Precision.HIGHEST
    own_block = lax.all_gather(factor, "cuts", axis=0, tiled=True)
    block = own_block.shape[0]
    partner_block = swapped(own_block, "tile", 1)
    first_block = jnp.where(band_index == 0, own_block, partner_block)
    second_block = jnp.where(band_index == 0, partner_block, own_block)
    column_factor = jnp.concatenate([first_block, second_block], 0)
    window_block = from_root(own_block, "tile", 0)
    window_rows = lax.dynamic_slice_in_dim(window_block, band_index * rows_band, rows_band, 0)
    window32 = window_rows.astype(F32)
    coef = 1.0 / math.sqrt(months * n_cuts * window_size)
    acc_columns = jnp.zeros((2 * block, P_SIZE), F32)
    acc_window = jnp.zeros((rows_band, P_SIZE), F32)
    acc_core = jnp.zeros((P_SIZE, P_SIZE), F32)
    diag_terms = []
    for month in range(months):
        diag_k = scales[month]
        inner = diag_k[:, None] * core * diag_k[None, :]
        mapped = jnp.dot(window32, inner, precision=highest).astype(BF16)
        model = dot(mapped, column_factor, NT)
        residual = (trade[month, 0].astype(F32) - model).astype(BF16)
        acc_columns = acc_columns + dot(residual, mapped, TN)
        projected = dot(residual, column_factor, NN)
        acc_window = acc_window + jnp.dot(projected, inner.T, precision=highest)
        gram = jnp.dot(window32.T, projected, precision=highest)
        acc_core = acc_core + diag_k[:, None] * gram * diag_k[None, :]
        weighted = gram * core
        diag_terms.append(
            jnp.dot(weighted, diag_k, precision=highest) + jnp.dot(weighted.T, diag_k, precision=highest)
        )
    diag_stack = jnp.stack(diag_terms, 0)
    halves = acc_columns.reshape(2, block, P_SIZE)
    mine = jnp.where(band_index == 0, halves[0], halves[1])
    theirs = jnp.where(band_index == 0, halves[1], halves[0])
    received = swapped(theirs, "tile", 1)
    grad_factor = lax.psum_scatter(mine + received, "cuts", scatter_dimension=0, tiled=True)
    padded = lax.dynamic_update_slice_in_dim(
        jnp.zeros((window_size, P_SIZE), F32), acc_window, band_index * rows_band, 0
    )
    window_part = lax.psum_scatter(padded, "cuts", scatter_dimension=0, tiled=True)
    window_total = lax.psum(window_part, "tile")
    core_total = lax.psum(acc_core, ("tile", "cuts"))
    diag_total = lax.psum(diag_stack, "tile")
    return (-coef * grad_factor, -coef * window_total, -coef * core_total, -coef * diag_total)


def body(trade, factor, scales, core):
    line = lax.axis_size("cuts") == 4 and lax.axis_size("tile") == 4
    if line and factor.shape[0] >= 2 * trade.shape[2]:
        return body_line(trade, factor, scales, core)
    return body_any(trade, factor, scales, core)


def solution(mesh):
    return jax.shard_map(
        body,
        mesh=mesh,
        in_specs=(
            P(("groups", "cuts"), "tile", None, None),
            P(("groups", "tile", "cuts"), None),
            P(("groups", "cuts"), None),
            P("groups", None),
        ),
        out_specs=(
            P(("groups", "tile", "cuts"), None),
            P(("groups", "cuts"), None),
            P("groups", None),
            P(("groups", "cuts"), None),
        ),
        check_vma=False,
    )
```

```python
import functools
import math

import jax
import jax.numpy as jnp
from jax import lax
from jax.experimental import pallas as pl
from jax.experimental.pallas import tpu as pltpu
from jax.sharding import PartitionSpec as P

P_SIZE = 256
F32, BF16, F16 = jnp.float32, jnp.bfloat16, jnp.float16
NN = (((1,), (0,)), ((), ()))
NT = (((1,), (1,)), ((), ()))
TN = (((0,), (0,)), ((), ()))
VMEM_LIMIT = 48 * 2**20
LARGE = pl.CostEstimate(flops=10**11, bytes_accessed=10**8, transcendentals=0)
SMALL = pl.CostEstimate(flops=1000, bytes_accessed=1000, transcendentals=0)


def dot(a, b, dims, **more):
    return lax.dot_general(a, b, dims, preferred_element_type=F32, **more)


def split3(value):
    first = value.astype(BF16)
    rest = value - first.astype(F32)
    second = rest.astype(BF16)
    return first, second, (rest - second.astype(F32)).astype(BF16)


def swapped(value, axis, mask):
    pairs = [(source, source ^ mask) for source in range(lax.axis_size(axis))]
    return lax.ppermute(value, axis, pairs)


def mapped_kernel(core_ref, window_ref, inner_ref, mapped_ref, turned_ref):
    rows = window_ref.shape[0] // 2
    at = core_ref[0]
    own = window_ref[pl.ds(pl.multiple_of(at * rows, rows), rows), :]
    other = window_ref[pl.ds(pl.multiple_of((1 - at) * rows, rows), rows), :]
    window = jnp.concatenate([own, other], 0)
    for month in range(inner_ref.shape[0]):
        value = sum(dot(window, term, NN) for term in split3(inner_ref[month]))
        rounded = value.astype(BF16)
        mapped_ref[month] = rounded
        turned_ref[:, month * 2 * rows : (month + 1) * 2 * rows] = rounded.astype(F32).T.astype(BF16)


def mapped_call(core_at, window, inner):
    months, size = inner.shape[0], window.shape[0]
    return pl.pallas_call(
        mapped_kernel,
        out_shape=[
            jax.ShapeDtypeStruct((months, size, P_SIZE), BF16),
            jax.ShapeDtypeStruct((P_SIZE, months * size), BF16),
        ],
        in_specs=[
            pl.BlockSpec(memory_space=pltpu.SMEM),
            pl.BlockSpec(memory_space=pltpu.VMEM),
            pl.BlockSpec(memory_space=pltpu.VMEM),
        ],
        out_specs=[pl.BlockSpec(memory_space=pltpu.VMEM)] * 2,
        compiler_params=pltpu.CompilerParams(vmem_limit_bytes=VMEM_LIMIT),
        cost_estimate=SMALL,
        name="mapped",
    )(core_at, window, inner)


def half_kernel(at_ref, trade_ref, out_ref):
    out_ref[...] = trade_ref[:, 0]


def half_call(at, trade, half):
    months, rows = trade.shape[0], trade.shape[2]
    width = min(1024, half)
    steps = half // width
    return pl.pallas_call(
        half_kernel,
        grid_spec=pltpu.PrefetchScalarGridSpec(
            num_scalar_prefetch=1,
            grid=(steps,),
            in_specs=[pl.BlockSpec((months, 1, rows, width), lambda j, s: (0, 0, 0, s[0] * steps + j))],
            out_specs=pl.BlockSpec((months, rows, width), lambda j, s: (0, 0, j)),
        ),
        out_shape=jax.ShapeDtypeStruct((months, rows, half), trade.dtype),
        compiler_params=pltpu.CompilerParams(vmem_limit_bytes=VMEM_LIMIT),
        cost_estimate=SMALL,
        name="half",
    )(at, trade)


def encoded(value):
    peak = jnp.max(jnp.abs(value), axis=0, keepdims=True)
    exponent = jnp.ceil(jnp.log2(jnp.maximum(peak, 1e-30)))
    return value * jnp.exp2(15.0 - exponent), jnp.broadcast_to(exponent, (16, value.shape[1]))


def piece_kernel(scaled, at_ref, own_ref, other_ref, first_ref, second_ref, mapped_ref, turned_ref, grad_ref, proj_ref):
    step, width = pl.program_id(0), own_ref.shape[3]
    block = jnp.where(step == 0, first_ref[...], second_ref[...])
    months, rows = mapped_ref.shape[0], mapped_ref.shape[1] // 2
    parts = []
    for month in range(months):
        for band in range(2):
            flows = own_ref[month, 0] if band == 0 else other_ref[month]
            model = dot(mapped_ref[month, band * rows : (band + 1) * rows, :], block, NT)
            parts.append((flows.astype(F32) - model).astype(BF16))
    residual = jnp.concatenate(parts, 0)
    grad = dot(turned_ref[...], residual, NN)
    at = pl.multiple_of(step * width, width)
    if scaled:
        value, exponent = encoded(grad)
        grad_ref[:P_SIZE, pl.ds(at, width)] = value
        grad_ref[P_SIZE:, pl.ds(at, width)] = exponent
    else:
        grad_ref[:, pl.ds(at, width)] = grad
    projected = dot(residual, block, NN).reshape(proj_ref.shape)

    @pl.when(step == 0)
    def _():
        proj_ref[...] = projected

    @pl.when(step > 0)
    def _():
        proj_ref[...] += projected


def piece_call(at, trade, other, blocks, mapped, turned, scaled, cost, label):
    months, size = mapped.shape[0], mapped.shape[1]
    rows, width = size // 2, blocks[0].shape[0]
    vmem = pl.BlockSpec(memory_space=pltpu.VMEM)
    spec = pltpu.PrefetchScalarGridSpec(
        num_scalar_prefetch=1,
        grid=(2,),
        in_specs=[
            pl.BlockSpec((months, 1, rows, width), lambda j, s: (0, 0, 0, s[0] * 2 + j)),
            pl.BlockSpec((months, rows, width), lambda j, s: (0, 0, s[1] * 2 + j)),
        ]
        + [vmem] * 4,
        out_specs=[vmem, vmem],
    )
    return pl.pallas_call(
        functools.partial(piece_kernel, scaled),
        grid_spec=spec,
        out_shape=[
            jax.ShapeDtypeStruct((P_SIZE + 16 if scaled else P_SIZE, 2 * width), F32),
            jax.ShapeDtypeStruct((months, size, P_SIZE), F32),
        ],
        compiler_params=pltpu.CompilerParams(vmem_limit_bytes=VMEM_LIMIT),
        cost_estimate=cost,
        name=label,
    )(at, trade, other, *blocks, mapped, turned)


def final_kernel(coef, own_ref, *rest):
    received, out_ref = rest[:-1], rest[-1]
    total = own_ref[...]
    for ref in received:
        total = total + ref[:P_SIZE, :] * jnp.exp2(ref[P_SIZE : P_SIZE + 1, :] - 15.0)
    out_ref[...] = (-coef * total).T


def final_call(coef, own, received):
    columns = own.shape[1]
    width = columns // 2
    tall = pl.BlockSpec((P_SIZE + 16, width), lambda j: (0, j))
    return pl.pallas_call(
        functools.partial(final_kernel, coef),
        grid=(2,),
        in_specs=[pl.BlockSpec((P_SIZE, width), lambda j: (0, j))] + [tall] * len(received),
        out_specs=pl.BlockSpec((width, P_SIZE), lambda j: (j, 0)),
        out_shape=jax.ShapeDtypeStruct((columns, P_SIZE), F32),
        compiler_params=pltpu.CompilerParams(vmem_limit_bytes=VMEM_LIMIT),
        cost_estimate=SMALL,
        name="final",
    )(own, *received)


def terms_kernel(cuts, at_ref, window_ref, inner_ref, core_ref, scales_ref, columns_ref, *rest):
    projs, (keep_ref, send_ref, acc_ref) = rest[:-3], rest[-3:]
    months, size = projs[0].shape[0], projs[0].shape[1]
    rows = size // 2
    at = at_ref[0]
    own = window_ref[pl.ds(pl.multiple_of(at * rows, rows), rows), :]
    other = window_ref[pl.ds(pl.multiple_of((1 - at) * rows, rows), rows), :]
    window = jnp.concatenate([own, other], 0)
    core = core_ref[...]
    acc_window = jnp.zeros((size, P_SIZE), F32)
    acc_core = jnp.zeros((P_SIZE, P_SIZE), F32)
    diagonals = []
    for month in range(months):
        proj = projs[0][month]
        for ref in projs[1:]:
            proj = proj + ref[month]
        acc_window = acc_window + dot(proj, inner_ref[month], NT, precision=lax.Precision.HIGHEST)
        gram = sum(dot(window, term, TN) for term in split3(proj))
        down = columns_ref[:, month : month + 1]
        acc_core = acc_core + down * gram * scales_ref[month : month + 1, :]
        weighted = gram * core
        diagonals.append(jnp.sum((weighted + weighted.T) * down, axis=0, keepdims=True))
    diagonals.append(jnp.zeros((8 - months, P_SIZE), F32))
    diagonal = jnp.concatenate(diagonals, 0)
    acc_ref[pl.ds(pl.multiple_of(at * rows, rows), rows), :] = acc_window[:rows]
    acc_ref[pl.ds(pl.multiple_of((1 - at) * rows, rows), rows), :] = acc_window[rows:]
    acc_ref[size:, :] = acc_core
    w = size // (4 * cuts)
    q = P_SIZE // 4
    half = cuts * w + q
    for ref, which in ((keep_ref, at), (send_ref, 1 - at)):
        for x in range(2):
            for cut in range(cuts):
                start = pl.multiple_of(cut * 4 * w + which * 2 * w + x * w, 8)
                ref[x * half + cut * w : x * half + (cut + 1) * w, :] = acc_ref[pl.ds(start, w), :]
            start = pl.multiple_of(size + which * 2 * q + x * q, 8)
            ref[x * half + cuts * w : (x + 1) * half, :] = acc_ref[pl.ds(start, q), :]
        ref[2 * half :, :] = diagonal


def terms_call(cuts, core_at, window, inner, core, scales, projs):
    months, size = projs[0].shape[0], projs[0].shape[1]
    high = size // 2 + P_SIZE // 2 + 8
    vmem = pl.BlockSpec(memory_space=pltpu.VMEM)
    return pl.pallas_call(
        functools.partial(terms_kernel, cuts),
        in_specs=[pl.BlockSpec(memory_space=pltpu.SMEM)] + [vmem] * (5 + len(projs)),
        out_specs=[vmem, vmem],
        out_shape=[jax.ShapeDtypeStruct((high, P_SIZE), F32)] * 2,
        scratch_shapes=[pltpu.VMEM((size + P_SIZE, P_SIZE), F32)],
        compiler_params=pltpu.CompilerParams(vmem_limit_bytes=VMEM_LIMIT),
        cost_estimate=SMALL,
        name="terms",
    )(core_at, window, inner, core, scales, scales.T, *projs)


def body_line(trade, factor, scales, core):
    cuts = lax.axis_size("cuts")
    tile, cut = lax.axis_index("tile"), lax.axis_index("cuts")
    x, at = tile // 2, tile % 2
    months, rows = trade.shape[0], trade.shape[2]
    size, piece = 2 * rows, factor.shape[0]
    coef = 1.0 / math.sqrt(months * cuts * size)
    core_at = at.astype(jnp.int32).reshape(1)
    inner = scales[:, :, None] * core[None] * scales[:, None, :]
    hold = lax.optimization_barrier

    half = cuts * piece
    give = half_call((1 - at).astype(jnp.int32).reshape(1), trade, half)
    other = swapped(give, "tile", 1)

    parts = [factor[:size], factor[size:]]
    third = lax.ppermute(parts[0], ("tile", "cuts"), [(0, 3)])
    middle = [swapped(value, "cuts", 2) for value in parts]
    near = [swapped(value, "cuts", 1) for value in parts]
    line = jnp.where(cut == 0, parts[0], jnp.where(cut == 1, near[0], jnp.where(cut == 2, middle[0], third)))
    out = [lax.ppermute(line, "tile", [(0, target)]) for target in (1, 2, 3)]
    out, middle[1] = hold((out, middle[1]))
    far = [swapped(value, "cuts", 1) for value in middle]
    window = jnp.where(tile == 0, line, sum(out[1:], out[0]))
    mapped, turned = mapped_call(core_at, window, inner)

    def piece_of(which, block, scaled, cost, label, after=None):
        where = jnp.stack([at * cuts + which, which]).astype(jnp.int32)
        if after is not None:
            where, _ = hold((where, after))
        return piece_call(where, trade, other, block, mapped, turned, scaled, cost, label)

    grad_middle, proj_middle = piece_of(cut ^ 2, middle, True, SMALL, "piece_middle")
    grad_middle = grad_middle.astype(F16)
    from_middle = swapped(grad_middle, "cuts", 2)
    grad_own, proj_own = piece_of(cut, parts, False, LARGE, "piece_own", grad_middle)
    grad_far, proj_far = piece_of(cut ^ 3, far, True, SMALL, "piece_far", proj_own)
    grad_far = grad_far.astype(F16)
    from_far = swapped(grad_far, "cuts", 3)
    grad_near, proj_near = piece_of(cut ^ 1, near, True, SMALL, "piece_near", grad_far)
    grad_near = grad_near.astype(F16)
    from_near = swapped(grad_near, "cuts", 1)

    keep, send = terms_call(cuts, core_at, window, inner, core, scales, [proj_near, proj_own, proj_middle, proj_far])
    send, from_middle = hold((swapped(send, "tile", 1), from_middle))
    both = keep + send
    w, q = size // (4 * cuts), P_SIZE // 4
    part = cuts * w + q
    low, high, diagonal = both[:part], both[part : 2 * part], both[2 * part :]
    keep = jnp.concatenate([jnp.where(x == 0, low, high), diagonal], 0)
    send = jnp.concatenate([jnp.where(x == 0, high, low), diagonal], 0)
    quarter = keep + swapped(send, "tile", 2)
    diagonal = quarter[part : part + months]
    core_part = quarter[cuts * w : part]

    def for_cut(which):
        return jnp.concatenate([lax.dynamic_slice_in_dim(quarter, which * w, w, 0), core_part], 0)

    total = for_cut(cut)
    for mask in range(1, cuts):
        total = total + swapped(for_cut(cut ^ mask), "cuts", mask)

    def joined_pair(mine, theirs, first):
        return jnp.where(first, mine, theirs), jnp.where(first, theirs, mine)

    first, second = joined_pair(total, swapped(total, "tile", 2), x == 0)
    line_total = jnp.concatenate([first[:w], second[:w], first[w:], second[w:]], 0)
    first, second = joined_pair(line_total, swapped(line_total, "tile", 1), at == 0)
    grad_window = jnp.concatenate([first[: 2 * w], second[: 2 * w]], 0)
    grad_core = jnp.concatenate([first[2 * w :], second[2 * w :]], 0)

    received = [value.astype(F32) for value in (from_near, from_middle, from_far)]
    grad_factor = final_call(coef, grad_own, received)
    return (grad_factor, -coef * grad_window, -coef * grad_core, -coef * diagonal)


def from_root(block, axis, source):
    block = jnp.where(lax.axis_index(axis) == source, block, jnp.zeros_like(block))
    return lax.psum(block, axis)


def body_any(trade, factor, scales, core):
    n_cuts = lax.axis_size("cuts")
    band_index = lax.axis_index("tile") % 2
    months = trade.shape[0]
    rows_band = trade.shape[2]
    window_size = 2 * rows_band
    highest = lax.Precision.HIGHEST
    own_block = lax.all_gather(factor, "cuts", axis=0, tiled=True)
    block = own_block.shape[0]
    partner_block = swapped(own_block, "tile", 1)
    first_block = jnp.where(band_index == 0, own_block, partner_block)
    second_block = jnp.where(band_index == 0, partner_block, own_block)
    column_factor = jnp.concatenate([first_block, second_block], 0)
    window_block = from_root(own_block, "tile", 0)
    window_rows = lax.dynamic_slice_in_dim(window_block, band_index * rows_band, rows_band, 0)
    window32 = window_rows.astype(F32)
    coef = 1.0 / math.sqrt(months * n_cuts * window_size)
    acc_columns = jnp.zeros((2 * block, P_SIZE), F32)
    acc_window = jnp.zeros((rows_band, P_SIZE), F32)
    acc_core = jnp.zeros((P_SIZE, P_SIZE), F32)
    diag_terms = []
    for month in range(months):
        diag_k = scales[month]
        inner = diag_k[:, None] * core * diag_k[None, :]
        mapped = jnp.dot(window32, inner, precision=highest).astype(BF16)
        model = dot(mapped, column_factor, NT)
        residual = (trade[month, 0].astype(F32) - model).astype(BF16)
        acc_columns = acc_columns + dot(residual, mapped, TN)
        projected = dot(residual, column_factor, NN)
        acc_window = acc_window + jnp.dot(projected, inner.T, precision=highest)
        gram = jnp.dot(window32.T, projected, precision=highest)
        acc_core = acc_core + diag_k[:, None] * gram * diag_k[None, :]
        weighted = gram * core
        diag_terms.append(
            jnp.dot(weighted, diag_k, precision=highest) + jnp.dot(weighted.T, diag_k, precision=highest)
        )
    diag_stack = jnp.stack(diag_terms, 0)
    halves = acc_columns.reshape(2, block, P_SIZE)
    mine = jnp.where(band_index == 0, halves[0], halves[1])
    theirs = jnp.where(band_index == 0, halves[1], halves[0])
    received = swapped(theirs, "tile", 1)
    grad_factor = lax.psum_scatter(mine + received, "cuts", scatter_dimension=0, tiled=True)
    padded = lax.dynamic_update_slice_in_dim(
        jnp.zeros((window_size, P_SIZE), F32), acc_window, band_index * rows_band, 0
    )
    window_part = lax.psum_scatter(padded, "cuts", scatter_dimension=0, tiled=True)
    window_total = lax.psum(window_part, "tile")
    core_total = lax.psum(acc_core, ("tile", "cuts"))
    diag_total = lax.psum(diag_stack, "tile")
    return (-coef * grad_factor, -coef * window_total, -coef * core_total, -coef * diag_total)


def body(trade, factor, scales, core):
    line = lax.axis_size("cuts") == 4 and lax.axis_size("tile") == 4
    if line and factor.shape[0] == 4 * trade.shape[2]:
        return body_line(trade, factor, scales, core)
    return body_any(trade, factor, scales, core)


def solution(mesh):
    return jax.shard_map(
        body,
        mesh=mesh,
        in_specs=(
            P(("groups", "cuts"), "tile", None, None),
            P(("groups", "tile", "cuts"), None),
            P(("groups", "cuts"), None),
            P("groups", None),
        ),
        out_specs=(
            P(("groups", "tile", "cuts"), None),
            P(("groups", "cuts"), None),
            P("groups", None),
            P(("groups", "cuts"), None),
        ),
        check_vma=False,
    )
```

```python
import functools
import math

import jax
import jax.numpy as jnp
from jax import lax
from jax.experimental import pallas as pl
from jax.experimental.pallas import tpu as pltpu
from jax.sharding import PartitionSpec as P

P_SIZE = 256
F32, BF16, F16 = jnp.float32, jnp.bfloat16, jnp.float16
NN = (((1,), (0,)), ((), ()))
NT = (((1,), (1,)), ((), ()))
TN = (((0,), (0,)), ((), ()))
VMEM_LIMIT = 48 * 2**20
LARGE = pl.CostEstimate(flops=10**11, bytes_accessed=10**8, transcendentals=0)
SMALL = pl.CostEstimate(flops=1000, bytes_accessed=1000, transcendentals=0)


def dot(a, b, dims, **more):
    return lax.dot_general(a, b, dims, preferred_element_type=F32, **more)


def split3(value):
    first = value.astype(BF16)
    rest = value - first.astype(F32)
    second = rest.astype(BF16)
    return first, second, (rest - second.astype(F32)).astype(BF16)


def swapped(value, axis, mask):
    pairs = [(source, source ^ mask) for source in range(lax.axis_size(axis))]
    return lax.ppermute(value, axis, pairs)


def mapped_kernel(core_ref, window_ref, inner_ref, mapped_ref, turned_ref):
    rows = window_ref.shape[0] // 2
    at = core_ref[0]
    own = window_ref[pl.ds(pl.multiple_of(at * rows, rows), rows), :]
    other = window_ref[pl.ds(pl.multiple_of((1 - at) * rows, rows), rows), :]
    window = jnp.concatenate([own, other], 0)
    for month in range(inner_ref.shape[0]):
        value = sum(dot(window, term, NN) for term in split3(inner_ref[month]))
        rounded = value.astype(BF16)
        mapped_ref[month] = rounded
        turned_ref[:, month * 2 * rows : (month + 1) * 2 * rows] = rounded.astype(F32).T.astype(BF16)


def mapped_call(core_at, window, inner):
    months, size = inner.shape[0], window.shape[0]
    return pl.pallas_call(
        mapped_kernel,
        out_shape=[
            jax.ShapeDtypeStruct((months, size, P_SIZE), BF16),
            jax.ShapeDtypeStruct((P_SIZE, months * size), BF16),
        ],
        in_specs=[
            pl.BlockSpec(memory_space=pltpu.SMEM),
            pl.BlockSpec(memory_space=pltpu.VMEM),
            pl.BlockSpec(memory_space=pltpu.VMEM),
        ],
        out_specs=[pl.BlockSpec(memory_space=pltpu.VMEM)] * 2,
        compiler_params=pltpu.CompilerParams(vmem_limit_bytes=VMEM_LIMIT),
        cost_estimate=SMALL,
        name="mapped",
    )(core_at, window, inner)


def half_kernel(at_ref, trade_ref, out_ref):
    out_ref[...] = trade_ref[:, 0]


def half_call(at, trade, half):
    months, rows = trade.shape[0], trade.shape[2]
    width = min(1024, half)
    steps = half // width
    return pl.pallas_call(
        half_kernel,
        grid_spec=pltpu.PrefetchScalarGridSpec(
            num_scalar_prefetch=1,
            grid=(steps,),
            in_specs=[pl.BlockSpec((months, 1, rows, width), lambda j, s: (0, 0, 0, s[0] * steps + j))],
            out_specs=pl.BlockSpec((months, rows, width), lambda j, s: (0, 0, j)),
        ),
        out_shape=jax.ShapeDtypeStruct((months, rows, half), trade.dtype),
        compiler_params=pltpu.CompilerParams(vmem_limit_bytes=VMEM_LIMIT),
        cost_estimate=LARGE,
        name="half",
    )(at, trade)


def encoded(value):
    peak = jnp.max(jnp.abs(value), axis=0, keepdims=True)
    exponent = jnp.ceil(jnp.log2(jnp.maximum(peak, 1e-30)))
    return value * jnp.exp2(15.0 - exponent), jnp.broadcast_to(exponent, (16, value.shape[1]))


def decoded(value):
    return value[:P_SIZE, :] * jnp.exp2(value[P_SIZE : P_SIZE + 1, :] - 15.0)


def piece_kernel(kind, chained, count, at_ref, own_ref, other_ref, *rest):
    blocks, (mapped_ref, turned_ref), rest = rest[:count], rest[count : count + 2], rest[count + 2 :]
    before_ref, outs = (rest[0], rest[1:]) if chained else (None, rest)
    grads, proj_ref = outs[:-1], outs[-1]
    step, width = pl.program_id(0), own_ref.shape[3]
    at = pl.multiple_of(step * width, width)
    if count == 1:
        block = blocks[0][pl.ds(at, width), :]
    else:
        block = jnp.where(step == 0, blocks[0][...], blocks[1][...])
    months, rows = mapped_ref.shape[0], mapped_ref.shape[1] // 2
    parts = []
    for month in range(months):
        for band in range(2):
            flows = own_ref[month, 0] if band == 0 else other_ref[month]
            model = dot(mapped_ref[month, band * rows : (band + 1) * rows, :], block, NT)
            parts.append((flows.astype(F32) - model).astype(BF16))
    residual = jnp.concatenate(parts, 0)
    grad = dot(turned_ref[...], residual, NN)
    if kind == "own":
        grads[0][:, pl.ds(at, width)] = grad
    else:
        value, exponent = encoded(grad)
        if kind == "whole":
            grads[0][:P_SIZE, pl.ds(at, width)] = value
            grads[0][P_SIZE:, pl.ds(at, width)] = exponent
        else:
            for index, ref in enumerate(grads):

                @pl.when(step == index)
                def _():
                    ref[:P_SIZE, :] = value
                    ref[P_SIZE:, :] = exponent

    projected = dot(residual, block, NN).reshape(proj_ref.shape)

    @pl.when(step == 0)
    def _():
        proj_ref[...] = before_ref[...] + projected if chained else projected

    @pl.when(step > 0)
    def _():
        proj_ref[...] += projected


def piece_call(at, trade, other, blocks, mapped, turned, before, kind, cost, label):
    months, size = mapped.shape[0], mapped.shape[1]
    rows, width = size // 2, sum(block.shape[0] for block in blocks) // 2
    vmem = pl.BlockSpec(memory_space=pltpu.VMEM)
    grads = {
        "own": [(P_SIZE, 2 * width)],
        "whole": [(P_SIZE + 16, 2 * width)],
        "split": [(P_SIZE + 16, width)] * 2,
    }[kind]
    spec = pltpu.PrefetchScalarGridSpec(
        num_scalar_prefetch=1,
        grid=(2,),
        in_specs=[
            pl.BlockSpec((months, 1, rows, width), lambda j, s: (0, 0, 0, s[0] * 2 + j)),
            pl.BlockSpec((months, rows, width), lambda j, s: (0, 0, s[1] * 2 + j)),
        ]
        + [vmem] * (2 + len(blocks) + len(before)),
        out_specs=[vmem] * (len(grads) + 1),
    )
    return pl.pallas_call(
        functools.partial(piece_kernel, kind, len(before) > 0, len(blocks)),
        grid_spec=spec,
        out_shape=[jax.ShapeDtypeStruct(shape, F32) for shape in grads]
        + [jax.ShapeDtypeStruct((months, size, P_SIZE), F32)],
        compiler_params=pltpu.CompilerParams(vmem_limit_bytes=VMEM_LIMIT),
        cost_estimate=cost,
        name=label,
    )(at, trade, other, *blocks, mapped, turned, *before)


def relay_kernel(received_ref, own_ref, *outs):
    step = pl.program_id(0)
    value, exponent = encoded(decoded(received_ref[...]) + own_ref[...])
    for index, ref in enumerate(outs):

        @pl.when(step == index)
        def _():
            ref[:P_SIZE, :] = value
            ref[P_SIZE:, :] = exponent


def relay_call(received, own):
    width = own.shape[1] // 2
    vmem = pl.BlockSpec(memory_space=pltpu.VMEM)
    return pl.pallas_call(
        relay_kernel,
        grid=(2,),
        in_specs=[
            pl.BlockSpec((P_SIZE + 16, width), lambda j: (0, j)),
            pl.BlockSpec((P_SIZE, width), lambda j: (0, j)),
        ],
        out_specs=[vmem, vmem],
        out_shape=[jax.ShapeDtypeStruct((P_SIZE + 16, width), F32)] * 2,
        compiler_params=pltpu.CompilerParams(vmem_limit_bytes=VMEM_LIMIT),
        cost_estimate=SMALL,
        name="relay",
    )(received, own)


def final_kernel(coef, own_ref, near_ref, first_ref, second_ref, out_ref):
    far = jnp.where(pl.program_id(0) == 0, first_ref[...], second_ref[...])
    total = own_ref[...] + decoded(near_ref[...]) + decoded(far)
    out_ref[...] = (-coef * total).T


def final_call(coef, own, near, halves):
    columns = own.shape[1]
    width = columns // 2
    vmem = pl.BlockSpec(memory_space=pltpu.VMEM)
    return pl.pallas_call(
        functools.partial(final_kernel, coef),
        grid=(2,),
        in_specs=[
            pl.BlockSpec((P_SIZE, width), lambda j: (0, j)),
            pl.BlockSpec((P_SIZE + 16, width), lambda j: (0, j)),
            vmem,
            vmem,
        ],
        out_specs=pl.BlockSpec((width, P_SIZE), lambda j: (j, 0)),
        out_shape=jax.ShapeDtypeStruct((columns, P_SIZE), F32),
        compiler_params=pltpu.CompilerParams(vmem_limit_bytes=VMEM_LIMIT),
        cost_estimate=SMALL,
        name="final",
    )(own, near, *halves)


def terms_kernel(cuts, at_ref, window_ref, inner_ref, core_ref, scales_ref, columns_ref, *rest):
    projs, outs, acc_ref = rest[:-5], rest[-5:-1], rest[-1]
    months, size = projs[0].shape[0], projs[0].shape[1]
    rows = size // 2
    tile, cut = at_ref[0], at_ref[1]
    at = tile % 2
    own = window_ref[pl.ds(pl.multiple_of(at * rows, rows), rows), :]
    other = window_ref[pl.ds(pl.multiple_of((1 - at) * rows, rows), rows), :]
    window = jnp.concatenate([own, other], 0)
    core = core_ref[...]
    acc_window = jnp.zeros((size, P_SIZE), F32)
    acc_core = jnp.zeros((P_SIZE, P_SIZE), F32)
    diagonals = []
    for month in range(months):
        proj = projs[0][month]
        for ref in projs[1:]:
            proj = proj + ref[month]
        acc_window = acc_window + dot(proj, inner_ref[month], NT, precision=lax.Precision.HIGHEST)
        gram = sum(dot(window, term, TN) for term in split3(proj))
        down = columns_ref[:, month : month + 1]
        acc_core = acc_core + down * gram * scales_ref[month : month + 1, :]
        weighted = gram * core
        diagonals.append(jnp.sum((weighted + weighted.T) * down, axis=0, keepdims=True))
    diagonals.append(jnp.zeros((8 - months, P_SIZE), F32))
    diagonal = jnp.concatenate(diagonals, 0)
    acc_ref[pl.ds(pl.multiple_of(at * rows, rows), rows), :] = acc_window[:rows]
    acc_ref[pl.ds(pl.multiple_of((1 - at) * rows, rows), rows), :] = acc_window[rows:]
    acc_ref[size:, :] = acc_core
    w, q = size // (4 * cuts), P_SIZE // 4
    for mask, ref in enumerate(outs):
        for turn in range(cuts):
            start = pl.multiple_of((cut ^ turn) * 4 * w + (tile ^ mask) * w, 8)
            ref[turn * w : (turn + 1) * w, :] = acc_ref[pl.ds(start, w), :]
        start = pl.multiple_of(size + (tile ^ mask) * q, 8)
        ref[cuts * w : cuts * w + q, :] = acc_ref[pl.ds(start, q), :]
        ref[cuts * w + q :, :] = diagonal


def terms_call(cuts, place, window, inner, core, scales, projs):
    months, size = projs[0].shape[0], projs[0].shape[1]
    high = size // 4 + P_SIZE // 4 + 8
    vmem = pl.BlockSpec(memory_space=pltpu.VMEM)
    return pl.pallas_call(
        functools.partial(terms_kernel, cuts),
        in_specs=[pl.BlockSpec(memory_space=pltpu.SMEM)] + [vmem] * (5 + len(projs)),
        out_specs=[vmem] * 4,
        out_shape=[jax.ShapeDtypeStruct((high, P_SIZE), F32)] * 4,
        scratch_shapes=[pltpu.VMEM((size + P_SIZE, P_SIZE), F32)],
        compiler_params=pltpu.CompilerParams(vmem_limit_bytes=VMEM_LIMIT),
        cost_estimate=SMALL,
        name="terms",
    )(place, window, inner, core, scales, scales.T, *projs)


def quarter_kernel(coef, cuts, months, own_ref, *rest):
    received, outs, diagonal_ref = rest[:3], rest[3:-1], rest[-1]
    total = own_ref[...]
    for ref in received:
        total = total + ref[...]
    w, q = (total.shape[0] - 8 - P_SIZE // 4) // cuts, P_SIZE // 4
    for turn, ref in enumerate(outs):
        ref[:w, :] = total[turn * w : (turn + 1) * w, :]
        ref[w:, :] = total[cuts * w : cuts * w + q, :]
    diagonal_ref[...] = -coef * total[cuts * w + q : cuts * w + q + months, :]


def quarter_call(coef, cuts, months, own, received):
    w, q = (own.shape[0] - 8 - P_SIZE // 4) // cuts, P_SIZE // 4
    vmem = pl.BlockSpec(memory_space=pltpu.VMEM)
    return pl.pallas_call(
        functools.partial(quarter_kernel, coef, cuts, months),
        in_specs=[vmem] * 4,
        out_specs=[vmem] * (cuts + 1),
        out_shape=[jax.ShapeDtypeStruct((w + q, P_SIZE), F32)] * cuts
        + [jax.ShapeDtypeStruct((months, P_SIZE), F32)],
        cost_estimate=SMALL,
        name="quarter",
    )(own, *received)


def join_kernel(coef, at_ref, *rest):
    parts, (window_ref, core_ref) = rest[:4], rest[4:]
    tile = at_ref[0]
    w, q = window_ref.shape[0] // 4, core_ref.shape[0] // 4
    for mask, ref in enumerate(parts):
        window_ref[pl.ds(pl.multiple_of((tile ^ mask) * w, 8), w), :] = -coef * ref[:w, :]
        core_ref[pl.ds(pl.multiple_of((tile ^ mask) * q, 8), q), :] = -coef * ref[w:, :]


def join_call(coef, place, parts):
    q = P_SIZE // 4
    w = parts[0].shape[0] - q
    vmem = pl.BlockSpec(memory_space=pltpu.VMEM)
    return pl.pallas_call(
        functools.partial(join_kernel, coef),
        in_specs=[pl.BlockSpec(memory_space=pltpu.SMEM)] + [vmem] * 4,
        out_specs=[vmem] * 2,
        out_shape=[jax.ShapeDtypeStruct((4 * w, P_SIZE), F32), jax.ShapeDtypeStruct((P_SIZE, P_SIZE), F32)],
        cost_estimate=SMALL,
        name="join",
    )(place, *parts)


def body_line(trade, factor, scales, core):
    cuts = lax.axis_size("cuts")
    tile, cut = lax.axis_index("tile"), lax.axis_index("cuts")
    at = tile % 2
    months, rows = trade.shape[0], trade.shape[2]
    size, piece = 2 * rows, factor.shape[0]
    coef = 1.0 / math.sqrt(months * cuts * size)
    place = jnp.stack([tile, cut]).astype(jnp.int32)
    core_at = at.astype(jnp.int32).reshape(1)
    inner = scales[:, :, None] * core[None] * scales[:, None, :]
    hold = lax.optimization_barrier

    half = cuts * piece
    give = half_call((1 - at).astype(jnp.int32).reshape(1), trade, half)

    parts = [factor[:size], factor[size:]]
    second = lax.ppermute(parts[0], ("tile", "cuts"), [(0, 2)])
    far = [swapped(value, "cuts", 3) for value in parts]
    near = [swapped(value, "cuts", 1) for value in parts]
    second, near[0], far[0], give = hold((second, near[0], far[0], give))
    first = near[0]
    other = swapped(give, "tile", 1)
    line = jnp.where(cut == 0, parts[0], jnp.where(cut == 1, first, jnp.where(cut == 2, second, far[0])))
    out = [lax.ppermute(line, "tile", [(0, target)]) for target in (1, 2, 3)]
    window = jnp.where(tile == 0, line, sum(out[1:], out[0]))
    mapped, turned = mapped_call(core_at, window, inner)

    def piece_of(which, blocks, kind, cost, label, before, after=None):
        where = jnp.stack([at * cuts + which, which]).astype(jnp.int32)
        if after is not None:
            where, _ = hold((where, after))
        return piece_call(where, trade, other, blocks, mapped, turned, before, kind, cost, label)

    grad_own, proj = piece_of(cut, [factor], "own", LARGE, "piece_own", [])
    far[1], _ = hold((far[1], proj))
    middle = [swapped(value, "cuts", 1) for value in far]
    grad_far, proj = piece_of(cut ^ 3, far, "whole", SMALL, "piece_far", [proj], proj)
    grad_far = grad_far.astype(F16)
    joined = swapped(grad_far, "cuts", 1)
    grad_near, proj = piece_of(cut ^ 1, near, "whole", LARGE, "piece_near", [proj], grad_far)
    grad_near = grad_near.astype(F16)
    from_near = swapped(grad_near, "cuts", 1)
    grad_middle, proj = piece_of(cut ^ 2, middle, "own", SMALL, "piece_middle", [proj], grad_near)

    own, *send = terms_call(cuts, place, window, inner, core, scales, [proj])
    joined, send[2] = hold((joined, send[2]))
    received = [swapped(value, "tile", mask + 1) for mask, value in enumerate(send)]
    passed = list(relay_call(joined.astype(F32), grad_middle))
    from_middle = swapped(passed[0].astype(F16), "cuts", 2)
    own, *send, grad_scales = quarter_call(coef, cuts, months, own, received)
    send, passed[1] = hold((send, passed[1]))
    from_middle_second = swapped(passed[1].astype(F16), "cuts", 2)
    send = [swapped(value, "cuts", mask + 1) for mask, value in enumerate(send)]
    send, from_near, from_middle = hold((send, from_near, from_middle))
    total = own + sum(send)
    quarters = [swapped(total, "tile", mask) for mask in (1, 2, 3)]
    grad_window, grad_core = join_call(coef, place, [total] + quarters)

    halves = [from_middle.astype(F32), from_middle_second.astype(F32)]
    grad_factor = final_call(coef, grad_own, from_near.astype(F32), halves)
    return (grad_factor, grad_window, grad_core, grad_scales)


def from_root(block, axis, source):
    block = jnp.where(lax.axis_index(axis) == source, block, jnp.zeros_like(block))
    return lax.psum(block, axis)


def body_any(trade, factor, scales, core):
    n_cuts = lax.axis_size("cuts")
    band_index = lax.axis_index("tile") % 2
    months = trade.shape[0]
    rows_band = trade.shape[2]
    window_size = 2 * rows_band
    highest = lax.Precision.HIGHEST
    own_block = lax.all_gather(factor, "cuts", axis=0, tiled=True)
    block = own_block.shape[0]
    partner_block = swapped(own_block, "tile", 1)
    first_block = jnp.where(band_index == 0, own_block, partner_block)
    second_block = jnp.where(band_index == 0, partner_block, own_block)
    column_factor = jnp.concatenate([first_block, second_block], 0)
    window_block = from_root(own_block, "tile", 0)
    window_rows = lax.dynamic_slice_in_dim(window_block, band_index * rows_band, rows_band, 0)
    window32 = window_rows.astype(F32)
    coef = 1.0 / math.sqrt(months * n_cuts * window_size)
    acc_columns = jnp.zeros((2 * block, P_SIZE), F32)
    acc_window = jnp.zeros((rows_band, P_SIZE), F32)
    acc_core = jnp.zeros((P_SIZE, P_SIZE), F32)
    diag_terms = []
    for month in range(months):
        diag_k = scales[month]
        inner = diag_k[:, None] * core * diag_k[None, :]
        mapped = jnp.dot(window32, inner, precision=highest).astype(BF16)
        model = dot(mapped, column_factor, NT)
        residual = (trade[month, 0].astype(F32) - model).astype(BF16)
        acc_columns = acc_columns + dot(residual, mapped, TN)
        projected = dot(residual, column_factor, NN)
        acc_window = acc_window + jnp.dot(projected, inner.T, precision=highest)
        gram = jnp.dot(window32.T, projected, precision=highest)
        acc_core = acc_core + diag_k[:, None] * gram * diag_k[None, :]
        weighted = gram * core
        diag_terms.append(
            jnp.dot(weighted, diag_k, precision=highest) + jnp.dot(weighted.T, diag_k, precision=highest)
        )
    diag_stack = jnp.stack(diag_terms, 0)
    halves = acc_columns.reshape(2, block, P_SIZE)
    mine = jnp.where(band_index == 0, halves[0], halves[1])
    theirs = jnp.where(band_index == 0, halves[1], halves[0])
    received = swapped(theirs, "tile", 1)
    grad_factor = lax.psum_scatter(mine + received, "cuts", scatter_dimension=0, tiled=True)
    padded = lax.dynamic_update_slice_in_dim(
        jnp.zeros((window_size, P_SIZE), F32), acc_window, band_index * rows_band, 0
    )
    window_part = lax.psum_scatter(padded, "cuts", scatter_dimension=0, tiled=True)
    window_total = lax.psum(window_part, "tile")
    core_total = lax.psum(acc_core, ("tile", "cuts"))
    diag_total = lax.psum(diag_stack, "tile")
    return (-coef * grad_factor, -coef * window_total, -coef * core_total, -coef * diag_total)


def body(trade, factor, scales, core):
    line = lax.axis_size("cuts") == 4 and lax.axis_size("tile") == 4
    if line and factor.shape[0] == 4 * trade.shape[2]:
        return body_line(trade, factor, scales, core)
    return body_any(trade, factor, scales, core)


def solution(mesh):
    return jax.shard_map(
        body,
        mesh=mesh,
        in_specs=(
            P(("groups", "cuts"), "tile", None, None),
            P(("groups", "tile", "cuts"), None),
            P(("groups", "cuts"), None),
            P("groups", None),
        ),
        out_specs=(
            P(("groups", "tile", "cuts"), None),
            P(("groups", "cuts"), None),
            P("groups", None),
            P(("groups", "cuts"), None),
        ),
        check_vma=False,
    )
```

```python
import functools
import math

import jax
import jax.numpy as jnp
from jax import lax
from jax.experimental import pallas as pl
from jax.experimental.pallas import tpu as pltpu
from jax.sharding import PartitionSpec as P

P_SIZE = 256
F32, BF16, F16 = jnp.float32, jnp.bfloat16, jnp.float16
NN = (((1,), (0,)), ((), ()))
NT = (((1,), (1,)), ((), ()))
TN = (((0,), (0,)), ((), ()))
VMEM_LIMIT = 48 * 2**20
VMEM_SMALL = 8 * 2**20
LARGE = pl.CostEstimate(flops=10**11, bytes_accessed=10**8, transcendentals=0)
SMALL = pl.CostEstimate(flops=1000, bytes_accessed=1000, transcendentals=0)


def dot(a, b, dims, **more):
    return lax.dot_general(a, b, dims, preferred_element_type=F32, **more)


def split3(value):
    first = value.astype(BF16)
    rest = value - first.astype(F32)
    second = rest.astype(BF16)
    return first, second, (rest - second.astype(F32)).astype(BF16)


def swapped(value, axis, mask):
    pairs = [(source, source ^ mask) for source in range(lax.axis_size(axis))]
    return lax.ppermute(value, axis, pairs)


def mapped_kernel(core_ref, window_ref, inner_ref, mapped_ref, turned_ref):
    rows = window_ref.shape[0] // 2
    at = core_ref[0]
    own = window_ref[pl.ds(pl.multiple_of(at * rows, rows), rows), :]
    other = window_ref[pl.ds(pl.multiple_of((1 - at) * rows, rows), rows), :]
    window = jnp.concatenate([own, other], 0)
    for month in range(inner_ref.shape[0]):
        value = sum(dot(window, term, NN) for term in split3(inner_ref[month]))
        rounded = value.astype(BF16)
        mapped_ref[month] = rounded
        turned_ref[:, month * 2 * rows : (month + 1) * 2 * rows] = rounded.astype(F32).T.astype(BF16)


def mapped_call(core_at, window, inner):
    months, size = inner.shape[0], window.shape[0]
    return pl.pallas_call(
        mapped_kernel,
        out_shape=[
            jax.ShapeDtypeStruct((months, size, P_SIZE), BF16),
            jax.ShapeDtypeStruct((P_SIZE, months * size), BF16),
        ],
        in_specs=[
            pl.BlockSpec(memory_space=pltpu.SMEM),
            pl.BlockSpec(memory_space=pltpu.VMEM),
            pl.BlockSpec(memory_space=pltpu.VMEM),
        ],
        out_specs=[pl.BlockSpec(memory_space=pltpu.VMEM)] * 2,
        compiler_params=pltpu.CompilerParams(vmem_limit_bytes=VMEM_LIMIT),
        cost_estimate=SMALL,
        name="mapped",
    )(core_at, window, inner)


def half_kernel(at_ref, trade_ref, out_ref):
    out_ref[...] = trade_ref[:, 0]


def half_call(at, trade, half):
    months, rows = trade.shape[0], trade.shape[2]
    width = min(1024, half)
    steps = half // width
    return pl.pallas_call(
        half_kernel,
        grid_spec=pltpu.PrefetchScalarGridSpec(
            num_scalar_prefetch=1,
            grid=(steps,),
            in_specs=[pl.BlockSpec((months, 1, rows, width), lambda j, s: (0, 0, 0, s[0] * steps + j))],
            out_specs=pl.BlockSpec((months, rows, width), lambda j, s: (0, 0, j)),
        ),
        out_shape=jax.ShapeDtypeStruct((months, rows, half), trade.dtype),
        compiler_params=pltpu.CompilerParams(vmem_limit_bytes=VMEM_LIMIT),
        cost_estimate=LARGE,
        name="half",
    )(at, trade)


def encoded(value):
    peak = jnp.max(jnp.abs(value), axis=0, keepdims=True)
    exponent = jnp.ceil(jnp.log2(jnp.maximum(peak, 1e-30)))
    return value * jnp.exp2(15.0 - exponent), jnp.broadcast_to(exponent, (16, value.shape[1]))


def decoded(value):
    return value[:P_SIZE, :] * jnp.exp2(value[P_SIZE : P_SIZE + 1, :] - 15.0)


def piece_kernel(kind, chained, count, at_ref, own_ref, other_ref, *rest):
    blocks, (mapped_ref, turned_ref), rest = rest[:count], rest[count : count + 2], rest[count + 2 :]
    before_ref, outs = (rest[0], rest[1:]) if chained else (None, rest)
    grads, proj_ref = outs[:-1], outs[-1]
    step, width = pl.program_id(0), own_ref.shape[3]
    at = pl.multiple_of(step * width, width)
    if count == 1:
        block = blocks[0][pl.ds(at, width), :]
    else:
        block = jnp.where(step == 0, blocks[0][...], blocks[1][...])
    months, rows = mapped_ref.shape[0], mapped_ref.shape[1] // 2
    parts = []
    for month in range(months):
        for band in range(2):
            flows = own_ref[month, 0] if band == 0 else other_ref[month]
            model = dot(mapped_ref[month, band * rows : (band + 1) * rows, :], block, NT)
            parts.append((flows.astype(F32) - model).astype(BF16))
    residual = jnp.concatenate(parts, 0)
    grad = dot(turned_ref[...], residual, NN)
    if kind == "own":
        grads[0][:, pl.ds(at, width)] = grad
    else:
        value, exponent = encoded(grad)
        if kind == "whole":
            grads[0][:P_SIZE, pl.ds(at, width)] = value
            grads[0][P_SIZE:, pl.ds(at, width)] = exponent
        else:
            for index, ref in enumerate(grads):

                @pl.when(step == index)
                def _():
                    ref[:P_SIZE, :] = value
                    ref[P_SIZE:, :] = exponent

    projected = dot(residual, block, NN).reshape(proj_ref.shape)

    @pl.when(step == 0)
    def _():
        proj_ref[...] = before_ref[...] + projected if chained else projected

    @pl.when(step > 0)
    def _():
        proj_ref[...] += projected


def piece_call(at, trade, other, blocks, mapped, turned, before, kind, cost, label):
    months, size = mapped.shape[0], mapped.shape[1]
    rows, width = size // 2, sum(block.shape[0] for block in blocks) // 2
    vmem = pl.BlockSpec(memory_space=pltpu.VMEM)
    grads = {
        "own": [(P_SIZE, 2 * width)],
        "whole": [(P_SIZE + 16, 2 * width)],
        "split": [(P_SIZE + 16, width)] * 2,
    }[kind]
    spec = pltpu.PrefetchScalarGridSpec(
        num_scalar_prefetch=1,
        grid=(2,),
        in_specs=[
            pl.BlockSpec((months, 1, rows, width), lambda j, s: (0, 0, 0, s[0] * 2 + j)),
            pl.BlockSpec((months, rows, width), lambda j, s: (0, 0, s[1] * 2 + j)),
        ]
        + [vmem] * (2 + len(blocks) + len(before)),
        out_specs=[vmem] * (len(grads) + 1),
    )
    return pl.pallas_call(
        functools.partial(piece_kernel, kind, len(before) > 0, len(blocks)),
        grid_spec=spec,
        out_shape=[jax.ShapeDtypeStruct(shape, F32) for shape in grads]
        + [jax.ShapeDtypeStruct((months, size, P_SIZE), F32)],
        compiler_params=pltpu.CompilerParams(vmem_limit_bytes=VMEM_LIMIT),
        cost_estimate=cost,
        name=label,
    )(at, trade, other, *blocks, mapped, turned, *before)


def relay_kernel(received_ref, own_ref, *outs):
    step = pl.program_id(0)
    value, exponent = encoded(decoded(received_ref[...]) + own_ref[...])
    for index, ref in enumerate(outs):

        @pl.when(step == index)
        def _():
            ref[:P_SIZE, :] = value
            ref[P_SIZE:, :] = exponent


def relay_call(received, own):
    width = own.shape[1] // 2
    vmem = pl.BlockSpec(memory_space=pltpu.VMEM)
    return pl.pallas_call(
        relay_kernel,
        grid=(2,),
        in_specs=[
            pl.BlockSpec((P_SIZE + 16, width), lambda j: (0, j)),
            pl.BlockSpec((P_SIZE, width), lambda j: (0, j)),
        ],
        out_specs=[vmem, vmem],
        out_shape=[jax.ShapeDtypeStruct((P_SIZE + 16, width), F32)] * 2,
        compiler_params=pltpu.CompilerParams(vmem_limit_bytes=VMEM_LIMIT),
        cost_estimate=SMALL,
        name="relay",
    )(received, own)


def final_kernel(coef, own_ref, near_ref, first_ref, second_ref, out_ref):
    far = jnp.where(pl.program_id(0) == 0, first_ref[...], second_ref[...])
    total = own_ref[...] + decoded(near_ref[...]) + decoded(far)
    out_ref[...] = (-coef * total).T


def final_call(coef, own, near, halves):
    columns = own.shape[1]
    width = columns // 2
    vmem = pl.BlockSpec(memory_space=pltpu.VMEM)
    return pl.pallas_call(
        functools.partial(final_kernel, coef),
        grid=(2,),
        in_specs=[
            pl.BlockSpec((P_SIZE, width), lambda j: (0, j)),
            pl.BlockSpec((P_SIZE + 16, width), lambda j: (0, j)),
            vmem,
            vmem,
        ],
        out_specs=pl.BlockSpec((width, P_SIZE), lambda j: (j, 0)),
        out_shape=jax.ShapeDtypeStruct((columns, P_SIZE), F32),
        compiler_params=pltpu.CompilerParams(vmem_limit_bytes=VMEM_LIMIT),
        cost_estimate=SMALL,
        name="final",
    )(own, near, *halves)


def terms_kernel(cuts, at_ref, window_ref, inner_ref, core_ref, scales_ref, columns_ref, *rest):
    projs, outs, acc_ref = rest[:-5], rest[-5:-1], rest[-1]
    months, size = projs[0].shape[0], projs[0].shape[1]
    rows = size // 2
    tile, cut = at_ref[0], at_ref[1]
    at = tile % 2
    own = window_ref[pl.ds(pl.multiple_of(at * rows, rows), rows), :]
    other = window_ref[pl.ds(pl.multiple_of((1 - at) * rows, rows), rows), :]
    window = jnp.concatenate([own, other], 0)
    core = core_ref[...]
    acc_window = jnp.zeros((size, P_SIZE), F32)
    acc_core = jnp.zeros((P_SIZE, P_SIZE), F32)
    diagonals = []
    for month in range(months):
        proj = projs[0][month]
        for ref in projs[1:]:
            proj = proj + ref[month]
        acc_window = acc_window + dot(proj, inner_ref[month], NT, precision=lax.Precision.HIGHEST)
        gram = sum(dot(window, term, TN) for term in split3(proj))
        down = columns_ref[:, month : month + 1]
        acc_core = acc_core + down * gram * scales_ref[month : month + 1, :]
        weighted = gram * core
        diagonals.append(jnp.sum((weighted + weighted.T) * down, axis=0, keepdims=True))
    diagonals.append(jnp.zeros((8 - months, P_SIZE), F32))
    diagonal = jnp.concatenate(diagonals, 0)
    acc_ref[pl.ds(pl.multiple_of(at * rows, rows), rows), :] = acc_window[:rows]
    acc_ref[pl.ds(pl.multiple_of((1 - at) * rows, rows), rows), :] = acc_window[rows:]
    acc_ref[size:, :] = acc_core
    w, q = size // (4 * cuts), P_SIZE // 4
    for mask, ref in enumerate(outs):
        for turn in range(cuts):
            start = pl.multiple_of((cut ^ turn) * 4 * w + (tile ^ mask) * w, 8)
            ref[turn * w : (turn + 1) * w, :] = acc_ref[pl.ds(start, w), :]
        start = pl.multiple_of(size + (tile ^ mask) * q, 8)
        ref[cuts * w : cuts * w + q, :] = acc_ref[pl.ds(start, q), :]
        ref[cuts * w + q :, :] = diagonal


def terms_call(cuts, place, window, inner, core, scales, projs):
    months, size = projs[0].shape[0], projs[0].shape[1]
    high = size // 4 + P_SIZE // 4 + 8
    vmem = pl.BlockSpec(memory_space=pltpu.VMEM)
    return pl.pallas_call(
        functools.partial(terms_kernel, cuts),
        in_specs=[pl.BlockSpec(memory_space=pltpu.SMEM)] + [vmem] * (5 + len(projs)),
        out_specs=[vmem] * 4,
        out_shape=[jax.ShapeDtypeStruct((high, P_SIZE), F32)] * 4,
        scratch_shapes=[pltpu.VMEM((size + P_SIZE, P_SIZE), F32)],
        compiler_params=pltpu.CompilerParams(vmem_limit_bytes=VMEM_LIMIT),
        cost_estimate=SMALL,
        name="terms",
    )(place, window, inner, core, scales, scales.T, *projs)


def quarter_kernel(cuts, own_ref, *rest):
    received, outs, diagonal_ref = rest[:3], rest[3:-1], rest[-1]
    total = own_ref[...]
    for ref in received:
        total = total + ref[...]
    w, q = (total.shape[0] - 8 - P_SIZE // 4) // cuts, P_SIZE // 4
    for turn, ref in enumerate(outs):
        ref[:w, :] = total[turn * w : (turn + 1) * w, :]
        ref[w:, :] = total[cuts * w : cuts * w + q, :]
    diagonal_ref[...] = total[cuts * w + q :, :]


def quarter_call(cuts, own, received):
    w, q = (own.shape[0] - 8 - P_SIZE // 4) // cuts, P_SIZE // 4
    vmem = pl.BlockSpec(memory_space=pltpu.VMEM)
    return pl.pallas_call(
        functools.partial(quarter_kernel, cuts),
        in_specs=[vmem] * 4,
        out_specs=[vmem] * (cuts + 1),
        out_shape=[jax.ShapeDtypeStruct((w + q, P_SIZE), F32)] * cuts
        + [jax.ShapeDtypeStruct((8, P_SIZE), F32)],
        compiler_params=pltpu.CompilerParams(vmem_limit_bytes=VMEM_SMALL),
        cost_estimate=SMALL,
        name="quarter",
    )(own, *received)


def join_kernel(coef, at_ref, *rest):
    parts, diagonal_ref, (window_ref, core_ref, scales_ref) = rest[:4], rest[4], rest[5:]
    tile = at_ref[0]
    w, q = window_ref.shape[0] // 4, core_ref.shape[0] // 4
    for mask, ref in enumerate(parts):
        window_ref[pl.ds(pl.multiple_of((tile ^ mask) * w, 8), w), :] = -coef * ref[:w, :]
        core_ref[pl.ds(pl.multiple_of((tile ^ mask) * q, 8), q), :] = -coef * ref[w:, :]
    scales_ref[...] = -coef * diagonal_ref[: scales_ref.shape[0], :]


def join_call(coef, months, place, parts, diagonal):
    q = P_SIZE // 4
    w = parts[0].shape[0] - q
    vmem = pl.BlockSpec(memory_space=pltpu.VMEM)
    return pl.pallas_call(
        functools.partial(join_kernel, coef),
        in_specs=[pl.BlockSpec(memory_space=pltpu.SMEM)] + [vmem] * 5,
        out_specs=[vmem] * 3,
        out_shape=[jax.ShapeDtypeStruct((high, P_SIZE), F32) for high in (4 * w, P_SIZE, months)],
        compiler_params=pltpu.CompilerParams(vmem_limit_bytes=VMEM_SMALL),
        cost_estimate=SMALL,
        name="join",
    )(place, *parts, diagonal)


def body_line(trade, factor, scales, core):
    cuts = lax.axis_size("cuts")
    tile, cut = lax.axis_index("tile"), lax.axis_index("cuts")
    at = tile % 2
    months, rows = trade.shape[0], trade.shape[2]
    size, piece = 2 * rows, factor.shape[0]
    coef = 1.0 / math.sqrt(months * cuts * size)
    place = jnp.stack([tile, cut]).astype(jnp.int32)
    core_at = at.astype(jnp.int32).reshape(1)
    inner = scales[:, :, None] * core[None] * scales[:, None, :]
    hold = lax.optimization_barrier

    half = cuts * piece
    give = half_call((1 - at).astype(jnp.int32).reshape(1), trade, half)

    parts = [factor[:size], factor[size:]]
    second = lax.ppermute(parts[0], ("tile", "cuts"), [(0, 2)])
    far = [swapped(value, "cuts", 3) for value in parts]
    near = [swapped(value, "cuts", 1) for value in parts]
    second, near[0], far[0], give = hold((second, near[0], far[0], give))
    first = near[0]
    other = swapped(give, "tile", 1)
    line = jnp.where(cut == 0, parts[0], jnp.where(cut == 1, first, jnp.where(cut == 2, second, far[0])))
    out = [lax.ppermute(line, "tile", [(0, target)]) for target in (1, 2, 3)]
    window = jnp.where(tile == 0, line, sum(out[1:], out[0]))
    mapped, turned = mapped_call(core_at, window, inner)

    def piece_of(which, blocks, kind, cost, label, before, after=None):
        where = jnp.stack([at * cuts + which, which]).astype(jnp.int32)
        if after is not None:
            where, _ = hold((where, after))
        return piece_call(where, trade, other, blocks, mapped, turned, before, kind, cost, label)

    grad_own, proj = piece_of(cut, [factor], "own", LARGE, "piece_own", [])
    far[1], _ = hold((far[1], proj))
    middle = [swapped(value, "cuts", 1) for value in far]
    grad_far, proj = piece_of(cut ^ 3, far, "whole", SMALL, "piece_far", [proj], proj)
    grad_far = grad_far.astype(F16)
    joined = swapped(grad_far, "cuts", 1)
    grad_near, proj = piece_of(cut ^ 1, near, "whole", LARGE, "piece_near", [proj], grad_far)
    grad_near = grad_near.astype(F16)
    from_near = swapped(grad_near, "cuts", 1)
    grad_middle, proj = piece_of(cut ^ 2, middle, "own", SMALL, "piece_middle", [proj], grad_near)

    own, *send = terms_call(cuts, place, window, inner, core, scales, [proj])
    received = [swapped(value, "tile", mask + 1) for mask, value in enumerate(send)]
    joined, received[0] = hold((joined, received[0]))
    passed = list(relay_call(joined.astype(F32), grad_middle))
    from_middle = swapped(passed[0].astype(F16), "cuts", 2)
    own, *send, diagonal = quarter_call(cuts, own, received)
    send, passed[1] = hold((send, passed[1]))
    from_middle_second = swapped(passed[1].astype(F16), "cuts", 2)
    send = [swapped(value, "cuts", mask + 1) for mask, value in enumerate(send)]
    send, from_near, from_middle = hold((send, from_near, from_middle))
    total = own + sum(send)
    quarters = [swapped(total, "tile", mask) for mask in (1, 2, 3)]
    halves = [from_middle.astype(F32), from_middle_second.astype(F32)]
    grad_factor = final_call(coef, grad_own, from_near.astype(F32), halves)
    quarters, grad_factor = hold((quarters, grad_factor))
    grad_window, grad_core, grad_scales = join_call(coef, months, place, [total] + quarters, diagonal)
    return (grad_factor, grad_window, grad_core, grad_scales)


def from_root(block, axis, source):
    block = jnp.where(lax.axis_index(axis) == source, block, jnp.zeros_like(block))
    return lax.psum(block, axis)


def body_any(trade, factor, scales, core):
    n_cuts = lax.axis_size("cuts")
    band_index = lax.axis_index("tile") % 2
    months = trade.shape[0]
    rows_band = trade.shape[2]
    window_size = 2 * rows_band
    highest = lax.Precision.HIGHEST
    own_block = lax.all_gather(factor, "cuts", axis=0, tiled=True)
    block = own_block.shape[0]
    partner_block = swapped(own_block, "tile", 1)
    first_block = jnp.where(band_index == 0, own_block, partner_block)
    second_block = jnp.where(band_index == 0, partner_block, own_block)
    column_factor = jnp.concatenate([first_block, second_block], 0)
    window_block = from_root(own_block, "tile", 0)
    window_rows = lax.dynamic_slice_in_dim(window_block, band_index * rows_band, rows_band, 0)
    window32 = window_rows.astype(F32)
    coef = 1.0 / math.sqrt(months * n_cuts * window_size)
    acc_columns = jnp.zeros((2 * block, P_SIZE), F32)
    acc_window = jnp.zeros((rows_band, P_SIZE), F32)
    acc_core = jnp.zeros((P_SIZE, P_SIZE), F32)
    diag_terms = []
    for month in range(months):
        diag_k = scales[month]
        inner = diag_k[:, None] * core * diag_k[None, :]
        mapped = jnp.dot(window32, inner, precision=highest).astype(BF16)
        model = dot(mapped, column_factor, NT)
        residual = (trade[month, 0].astype(F32) - model).astype(BF16)
        acc_columns = acc_columns + dot(residual, mapped, TN)
        projected = dot(residual, column_factor, NN)
        acc_window = acc_window + jnp.dot(projected, inner.T, precision=highest)
        gram = jnp.dot(window32.T, projected, precision=highest)
        acc_core = acc_core + diag_k[:, None] * gram * diag_k[None, :]
        weighted = gram * core
        diag_terms.append(
            jnp.dot(weighted, diag_k, precision=highest) + jnp.dot(weighted.T, diag_k, precision=highest)
        )
    diag_stack = jnp.stack(diag_terms, 0)
    halves = acc_columns.reshape(2, block, P_SIZE)
    mine = jnp.where(band_index == 0, halves[0], halves[1])
    theirs = jnp.where(band_index == 0, halves[1], halves[0])
    received = swapped(theirs, "tile", 1)
    grad_factor = lax.psum_scatter(mine + received, "cuts", scatter_dimension=0, tiled=True)
    padded = lax.dynamic_update_slice_in_dim(
        jnp.zeros((window_size, P_SIZE), F32), acc_window, band_index * rows_band, 0
    )
    window_part = lax.psum_scatter(padded, "cuts", scatter_dimension=0, tiled=True)
    window_total = lax.psum(window_part, "tile")
    core_total = lax.psum(acc_core, ("tile", "cuts"))
    diag_total = lax.psum(diag_stack, "tile")
    return (-coef * grad_factor, -coef * window_total, -coef * core_total, -coef * diag_total)


def body(trade, factor, scales, core):
    line = lax.axis_size("cuts") == 4 and lax.axis_size("tile") == 4
    if line and factor.shape[0] == 4 * trade.shape[2]:
        return body_line(trade, factor, scales, core)
    return body_any(trade, factor, scales, core)


def solution(mesh):
    return jax.shard_map(
        body,
        mesh=mesh,
        in_specs=(
            P(("groups", "cuts"), "tile", None, None),
            P(("groups", "tile", "cuts"), None),
            P(("groups", "cuts"), None),
            P("groups", None),
        ),
        out_specs=(
            P(("groups", "tile", "cuts"), None),
            P(("groups", "cuts"), None),
            P("groups", None),
            P(("groups", "cuts"), None),
        ),
        check_vma=False,
    )
```

```python
import functools
import math

import jax
import jax.numpy as jnp
from jax import lax
from jax.experimental import pallas as pl
from jax.experimental.pallas import tpu as pltpu
from jax.sharding import PartitionSpec as P

P_SIZE = 256
F32, BF16, F16 = jnp.float32, jnp.bfloat16, jnp.float16
NN = (((1,), (0,)), ((), ()))
NT = (((1,), (1,)), ((), ()))
TN = (((0,), (0,)), ((), ()))
VMEM_LIMIT = 48 * 2**20
VMEM_SMALL = 8 * 2**20
LARGE = pl.CostEstimate(flops=10**11, bytes_accessed=10**8, transcendentals=0)
SMALL = pl.CostEstimate(flops=1000, bytes_accessed=1000, transcendentals=0)


def dot(a, b, dims, **more):
    return lax.dot_general(a, b, dims, preferred_element_type=F32, **more)


def split3(value):
    first = value.astype(BF16)
    rest = value - first.astype(F32)
    second = rest.astype(BF16)
    return first, second, (rest - second.astype(F32)).astype(BF16)


def swapped(value, axis, mask):
    pairs = [(source, source ^ mask) for source in range(lax.axis_size(axis))]
    return lax.ppermute(value, axis, pairs)


def mapped_kernel(core_ref, window_ref, inner_ref, mapped_ref, turned_ref):
    rows = window_ref.shape[0] // 2
    at = core_ref[0]
    own = window_ref[pl.ds(pl.multiple_of(at * rows, rows), rows), :]
    other = window_ref[pl.ds(pl.multiple_of((1 - at) * rows, rows), rows), :]
    window = jnp.concatenate([own, other], 0)
    for month in range(inner_ref.shape[0]):
        value = sum(dot(window, term, NN) for term in split3(inner_ref[month]))
        rounded = value.astype(BF16)
        mapped_ref[month] = rounded
        turned_ref[:, month * 2 * rows : (month + 1) * 2 * rows] = rounded.astype(F32).T.astype(BF16)


def mapped_call(core_at, window, inner):
    months, size = inner.shape[0], window.shape[0]
    return pl.pallas_call(
        mapped_kernel,
        out_shape=[
            jax.ShapeDtypeStruct((months, size, P_SIZE), BF16),
            jax.ShapeDtypeStruct((P_SIZE, months * size), BF16),
        ],
        in_specs=[
            pl.BlockSpec(memory_space=pltpu.SMEM),
            pl.BlockSpec(memory_space=pltpu.VMEM),
            pl.BlockSpec(memory_space=pltpu.VMEM),
        ],
        out_specs=[pl.BlockSpec(memory_space=pltpu.VMEM)] * 2,
        compiler_params=pltpu.CompilerParams(vmem_limit_bytes=VMEM_SMALL),
        cost_estimate=SMALL,
        name="mapped",
    )(core_at, window, inner)


def half_kernel(at_ref, trade_ref, out_ref):
    out_ref[...] = trade_ref[:, 0]


def half_call(at, trade, half):
    months, rows = trade.shape[0], trade.shape[2]
    width = min(1024, half)
    steps = half // width
    return pl.pallas_call(
        half_kernel,
        grid_spec=pltpu.PrefetchScalarGridSpec(
            num_scalar_prefetch=1,
            grid=(steps,),
            in_specs=[pl.BlockSpec((months, 1, rows, width), lambda j, s: (0, 0, 0, s[0] * steps + j))],
            out_specs=pl.BlockSpec((months, rows, width), lambda j, s: (0, 0, j)),
        ),
        out_shape=jax.ShapeDtypeStruct((months, rows, half), trade.dtype),
        compiler_params=pltpu.CompilerParams(vmem_limit_bytes=VMEM_LIMIT),
        cost_estimate=LARGE,
        name="half",
    )(at, trade)


def encoded(value):
    peak = jnp.max(jnp.abs(value), axis=0, keepdims=True)
    exponent = jnp.ceil(jnp.log2(jnp.maximum(peak, 1e-30)))
    return value * jnp.exp2(15.0 - exponent), jnp.broadcast_to(exponent, (16, value.shape[1]))


def decoded(value):
    return value[:P_SIZE, :] * jnp.exp2(value[P_SIZE : P_SIZE + 1, :] - 15.0)


def piece_kernel(kind, chained, count, at_ref, own_ref, other_ref, *rest):
    blocks, (mapped_ref, turned_ref), rest = rest[:count], rest[count : count + 2], rest[count + 2 :]
    before_ref, outs = (rest[0], rest[1:]) if chained else (None, rest)
    grads, proj_ref = outs[:-1], outs[-1]
    step, width = pl.program_id(0), own_ref.shape[3]
    at = pl.multiple_of(step * width, width)
    if count == 1:
        block = blocks[0][pl.ds(at, width), :]
    else:
        block = jnp.where(step == 0, blocks[0][...], blocks[1][...])
    months, rows = mapped_ref.shape[0], mapped_ref.shape[1] // 2
    parts = []
    for month in range(months):
        for band in range(2):
            flows = own_ref[month, 0] if band == 0 else other_ref[month]
            model = dot(mapped_ref[month, band * rows : (band + 1) * rows, :], block, NT)
            parts.append((flows.astype(F32) - model).astype(BF16))
    residual = jnp.concatenate(parts, 0)
    grad = dot(turned_ref[...], residual, NN)
    if kind == "plain":
        grads[0][:, pl.ds(at, width)] = grad
    else:
        value, exponent = encoded(grad)
        grads[0][:P_SIZE, pl.ds(at, width)] = value
        grads[0][P_SIZE:, pl.ds(at, width)] = exponent
    projected = dot(residual, block, NN).reshape(proj_ref.shape)

    @pl.when(step == 0)
    def _():
        proj_ref[...] = before_ref[...] + projected if chained else projected

    @pl.when(step > 0)
    def _():
        proj_ref[...] += projected


def piece_call(at, trade, other, blocks, mapped, turned, before, kind, cost, label):
    months, size = mapped.shape[0], mapped.shape[1]
    rows, width = size // 2, sum(block.shape[0] for block in blocks) // 2
    vmem = pl.BlockSpec(memory_space=pltpu.VMEM)
    grads = {
        "plain": [(P_SIZE, 2 * width)],
        "coded": [(P_SIZE + 16, 2 * width)],
    }[kind]
    spec = pltpu.PrefetchScalarGridSpec(
        num_scalar_prefetch=1,
        grid=(2,),
        in_specs=[
            pl.BlockSpec((months, 1, rows, width), lambda j, s: (0, 0, 0, s[0] * 2 + j)),
            pl.BlockSpec((months, rows, width), lambda j, s: (0, 0, s[1] * 2 + j)),
        ]
        + [vmem] * (2 + len(blocks) + len(before)),
        out_specs=[vmem] * (len(grads) + 1),
    )
    return pl.pallas_call(
        functools.partial(piece_kernel, kind, len(before) > 0, len(blocks)),
        grid_spec=spec,
        out_shape=[jax.ShapeDtypeStruct(shape, F32) for shape in grads]
        + [jax.ShapeDtypeStruct((months, size, P_SIZE), F32)],
        compiler_params=pltpu.CompilerParams(vmem_limit_bytes=VMEM_LIMIT),
        cost_estimate=cost,
        name=label,
    )(at, trade, other, *blocks, mapped, turned, *before)


def relay_kernel(received_ref, own_ref, *outs):
    step = pl.program_id(0)
    value, exponent = encoded(decoded(received_ref[...]) + own_ref[...])
    for index, ref in enumerate(outs):

        @pl.when(step == index)
        def _():
            ref[:P_SIZE, :] = value
            ref[P_SIZE:, :] = exponent


def relay_call(received, own):
    width = own.shape[1] // 2
    vmem = pl.BlockSpec(memory_space=pltpu.VMEM)
    return pl.pallas_call(
        relay_kernel,
        grid=(2,),
        in_specs=[
            pl.BlockSpec((P_SIZE + 16, width), lambda j: (0, j)),
            pl.BlockSpec((P_SIZE, width), lambda j: (0, j)),
        ],
        out_specs=[vmem, vmem],
        out_shape=[jax.ShapeDtypeStruct((P_SIZE + 16, width), F32)] * 2,
        compiler_params=pltpu.CompilerParams(vmem_limit_bytes=VMEM_SMALL),
        cost_estimate=SMALL,
        name="relay",
    )(received, own)


def final_kernel(coef, own_ref, near_ref, first_ref, second_ref, out_ref):
    far = jnp.where(pl.program_id(0) == 0, first_ref[...], second_ref[...])
    total = own_ref[...] + decoded(near_ref[...]) + decoded(far)
    out_ref[...] = (-coef * total).T


def final_call(coef, own, near, halves):
    columns = own.shape[1]
    width = columns // 2
    vmem = pl.BlockSpec(memory_space=pltpu.VMEM)
    return pl.pallas_call(
        functools.partial(final_kernel, coef),
        grid=(2,),
        in_specs=[
            pl.BlockSpec((P_SIZE, width), lambda j: (0, j)),
            pl.BlockSpec((P_SIZE + 16, width), lambda j: (0, j)),
            vmem,
            vmem,
        ],
        out_specs=pl.BlockSpec((width, P_SIZE), lambda j: (j, 0)),
        out_shape=jax.ShapeDtypeStruct((columns, P_SIZE), F32),
        compiler_params=pltpu.CompilerParams(vmem_limit_bytes=VMEM_SMALL),
        cost_estimate=SMALL,
        name="final",
    )(own, near, *halves)


def terms_kernel(cuts, at_ref, window_ref, inner_ref, core_ref, scales_ref, columns_ref, *rest):
    projs, outs, acc_ref = rest[:-5], rest[-5:-1], rest[-1]
    months, size = projs[0].shape[0], projs[0].shape[1]
    rows = size // 2
    tile, cut = at_ref[0], at_ref[1]
    at = tile % 2
    own = window_ref[pl.ds(pl.multiple_of(at * rows, rows), rows), :]
    other = window_ref[pl.ds(pl.multiple_of((1 - at) * rows, rows), rows), :]
    window = jnp.concatenate([own, other], 0)
    core = core_ref[...]
    acc_window = jnp.zeros((size, P_SIZE), F32)
    acc_core = jnp.zeros((P_SIZE, P_SIZE), F32)
    diagonals = []
    for month in range(months):
        proj = projs[0][month]
        for ref in projs[1:]:
            proj = proj + ref[month]
        acc_window = acc_window + dot(proj, inner_ref[month], NT, precision=lax.Precision.HIGHEST)
        gram = sum(dot(window, term, TN) for term in split3(proj))
        down = columns_ref[:, month : month + 1]
        acc_core = acc_core + down * gram * scales_ref[month : month + 1, :]
        weighted = gram * core
        diagonals.append(jnp.sum((weighted + weighted.T) * down, axis=0, keepdims=True))
    diagonals.append(jnp.zeros((8 - months, P_SIZE), F32))
    diagonal = jnp.concatenate(diagonals, 0)
    acc_ref[pl.ds(pl.multiple_of(at * rows, rows), rows), :] = acc_window[:rows]
    acc_ref[pl.ds(pl.multiple_of((1 - at) * rows, rows), rows), :] = acc_window[rows:]
    acc_ref[size:, :] = acc_core
    w, q = size // (4 * cuts), P_SIZE // 4
    for mask, ref in enumerate(outs):
        for turn in range(cuts):
            start = pl.multiple_of((cut ^ turn) * 4 * w + (tile ^ mask) * w, 8)
            ref[turn * w : (turn + 1) * w, :] = acc_ref[pl.ds(start, w), :]
        start = pl.multiple_of(size + (tile ^ mask) * q, 8)
        ref[cuts * w : cuts * w + q, :] = acc_ref[pl.ds(start, q), :]
        ref[cuts * w + q :, :] = diagonal


def terms_call(cuts, place, window, inner, core, scales, projs):
    months, size = projs[0].shape[0], projs[0].shape[1]
    high = size // 4 + P_SIZE // 4 + 8
    vmem = pl.BlockSpec(memory_space=pltpu.VMEM)
    return pl.pallas_call(
        functools.partial(terms_kernel, cuts),
        in_specs=[pl.BlockSpec(memory_space=pltpu.SMEM)] + [vmem] * (5 + len(projs)),
        out_specs=[vmem] * 4,
        out_shape=[jax.ShapeDtypeStruct((high, P_SIZE), F32)] * 4,
        scratch_shapes=[pltpu.VMEM((size + P_SIZE, P_SIZE), F32)],
        compiler_params=pltpu.CompilerParams(vmem_limit_bytes=VMEM_SMALL),
        cost_estimate=SMALL,
        name="terms",
    )(place, window, inner, core, scales, scales.T, *projs)


def quarter_kernel(cuts, own_ref, *rest):
    received, outs, diagonal_ref = rest[:3], rest[3:-1], rest[-1]
    total = own_ref[...]
    for ref in received:
        total = total + ref[...]
    w, q = (total.shape[0] - 8 - P_SIZE // 4) // cuts, P_SIZE // 4
    for turn, ref in enumerate(outs):
        ref[:w, :] = total[turn * w : (turn + 1) * w, :]
        ref[w:, :] = total[cuts * w : cuts * w + q, :]
    diagonal_ref[...] = total[cuts * w + q :, :]


def quarter_call(cuts, own, received):
    w, q = (own.shape[0] - 8 - P_SIZE // 4) // cuts, P_SIZE // 4
    vmem = pl.BlockSpec(memory_space=pltpu.VMEM)
    return pl.pallas_call(
        functools.partial(quarter_kernel, cuts),
        in_specs=[vmem] * 4,
        out_specs=[vmem] * (cuts + 1),
        out_shape=[jax.ShapeDtypeStruct((w + q, P_SIZE), F32)] * cuts
        + [jax.ShapeDtypeStruct((8, P_SIZE), F32)],
        compiler_params=pltpu.CompilerParams(vmem_limit_bytes=VMEM_SMALL),
        cost_estimate=SMALL,
        name="quarter",
    )(own, *received)


def join_kernel(coef, at_ref, *rest):
    parts, diagonal_ref, (window_ref, core_ref, scales_ref) = rest[:4], rest[4], rest[5:]
    tile = at_ref[0]
    w, q = window_ref.shape[0] // 4, core_ref.shape[0] // 4
    for mask, ref in enumerate(parts):
        window_ref[pl.ds(pl.multiple_of((tile ^ mask) * w, 8), w), :] = -coef * ref[:w, :]
        core_ref[pl.ds(pl.multiple_of((tile ^ mask) * q, 8), q), :] = -coef * ref[w:, :]
    scales_ref[...] = -coef * diagonal_ref[: scales_ref.shape[0], :]


def join_call(coef, months, place, parts, diagonal):
    q = P_SIZE // 4
    w = parts[0].shape[0] - q
    vmem = pl.BlockSpec(memory_space=pltpu.VMEM)
    return pl.pallas_call(
        functools.partial(join_kernel, coef),
        in_specs=[pl.BlockSpec(memory_space=pltpu.SMEM)] + [vmem] * 5,
        out_specs=[vmem] * 3,
        out_shape=[jax.ShapeDtypeStruct((high, P_SIZE), F32) for high in (4 * w, P_SIZE, months)],
        compiler_params=pltpu.CompilerParams(vmem_limit_bytes=VMEM_SMALL),
        cost_estimate=SMALL,
        name="join",
    )(place, *parts, diagonal)


def body_line(trade, factor, scales, core):
    cuts = lax.axis_size("cuts")
    tile, cut = lax.axis_index("tile"), lax.axis_index("cuts")
    at = tile % 2
    months, rows = trade.shape[0], trade.shape[2]
    size, piece = 2 * rows, factor.shape[0]
    coef = 1.0 / math.sqrt(months * cuts * size)
    place = jnp.stack([tile, cut]).astype(jnp.int32)
    core_at = at.astype(jnp.int32).reshape(1)
    inner = scales[:, :, None] * core[None] * scales[:, None, :]
    hold = lax.optimization_barrier

    half = cuts * piece
    give = half_call((1 - at).astype(jnp.int32).reshape(1), trade, half)

    parts = [factor[:size], factor[size:]]
    second = lax.ppermute(parts[0], ("tile", "cuts"), [(0, 2)])
    far = [swapped(value, "cuts", 3) for value in parts]
    near = [swapped(value, "cuts", 1) for value in parts]
    second, near[0], far[0], give = hold((second, near[0], far[0], give))
    other = swapped(give, "tile", 1)
    line = jnp.where(cut == 0, parts[0], jnp.where(cut == 1, near[0], jnp.where(cut == 2, second, far[0])))
    out = [lax.ppermute(line, "tile", [(0, target)]) for target in (3, 2, 1)]
    window = jnp.where(tile == 0, line, sum(out[1:], out[0]))
    mapped, turned = mapped_call(core_at, window, inner)

    def piece_of(which, blocks, kind, cost, label, before, after=None):
        where = jnp.stack([at * cuts + which, which]).astype(jnp.int32)
        if after is not None:
            where, _ = hold((where, after))
        return piece_call(where, trade, other, blocks, mapped, turned, before, kind, cost, label)

    grad_own, proj = piece_of(cut, [factor], "plain", LARGE, "piece_own", [])
    far[1], _ = hold((far[1], proj))
    middle = [swapped(value, "cuts", 1) for value in far]
    grad_far, proj = piece_of(cut ^ 3, far, "coded", SMALL, "piece_far", [proj], proj)
    grad_far = grad_far.astype(F16)
    joined = swapped(grad_far, "cuts", 1)
    grad_near, proj = piece_of(cut ^ 1, near, "coded", LARGE, "piece_near", [proj], grad_far)
    grad_near = grad_near.astype(F16)
    from_near = swapped(grad_near, "cuts", 1)
    grad_middle, proj = piece_of(cut ^ 2, middle, "plain", SMALL, "piece_middle", [proj], grad_near)

    own, *send = terms_call(cuts, place, window, inner, core, scales, [proj])
    received = [swapped(value, "tile", mask + 1) for mask, value in enumerate(send)]
    joined, received[0] = hold((joined, received[0]))
    passed = list(relay_call(joined.astype(F32), grad_middle))
    from_middle = swapped(passed[0].astype(F16), "cuts", 2)
    own, *send, diagonal = quarter_call(cuts, own, received)
    send, passed[1] = hold((send, passed[1]))
    from_middle_second = swapped(passed[1].astype(F16), "cuts", 2)
    send = [swapped(value, "cuts", mask + 1) for mask, value in enumerate(send)]
    send, from_near, from_middle = hold((send, from_near, from_middle))
    total = own + sum(send)
    quarters = [swapped(total, "tile", mask) for mask in (1, 2, 3)]
    halves = [from_middle.astype(F32), from_middle_second.astype(F32)]
    grad_factor = final_call(coef, grad_own, from_near.astype(F32), halves)
    quarters, grad_factor = hold((quarters, grad_factor))
    grad_window, grad_core, grad_scales = join_call(coef, months, place, [total] + quarters, diagonal)
    return (grad_factor, grad_window, grad_core, grad_scales)


def from_root(block, axis, source):
    block = jnp.where(lax.axis_index(axis) == source, block, jnp.zeros_like(block))
    return lax.psum(block, axis)


def body_any(trade, factor, scales, core):
    n_cuts = lax.axis_size("cuts")
    band_index = lax.axis_index("tile") % 2
    months = trade.shape[0]
    rows_band = trade.shape[2]
    window_size = 2 * rows_band
    highest = lax.Precision.HIGHEST
    own_block = lax.all_gather(factor, "cuts", axis=0, tiled=True)
    block = own_block.shape[0]
    partner_block = swapped(own_block, "tile", 1)
    first_block = jnp.where(band_index == 0, own_block, partner_block)
    second_block = jnp.where(band_index == 0, partner_block, own_block)
    column_factor = jnp.concatenate([first_block, second_block], 0)
    window_block = from_root(own_block, "tile", 0)
    window_rows = lax.dynamic_slice_in_dim(window_block, band_index * rows_band, rows_band, 0)
    window32 = window_rows.astype(F32)
    coef = 1.0 / math.sqrt(months * n_cuts * window_size)
    acc_columns = jnp.zeros((2 * block, P_SIZE), F32)
    acc_window = jnp.zeros((rows_band, P_SIZE), F32)
    acc_core = jnp.zeros((P_SIZE, P_SIZE), F32)
    diag_terms = []
    for month in range(months):
        diag_k = scales[month]
        inner = diag_k[:, None] * core * diag_k[None, :]
        mapped = jnp.dot(window32, inner, precision=highest).astype(BF16)
        model = dot(mapped, column_factor, NT)
        residual = (trade[month, 0].astype(F32) - model).astype(BF16)
        acc_columns = acc_columns + dot(residual, mapped, TN)
        projected = dot(residual, column_factor, NN)
        acc_window = acc_window + jnp.dot(projected, inner.T, precision=highest)
        gram = jnp.dot(window32.T, projected, precision=highest)
        acc_core = acc_core + diag_k[:, None] * gram * diag_k[None, :]
        weighted = gram * core
        diag_terms.append(
            jnp.dot(weighted, diag_k, precision=highest) + jnp.dot(weighted.T, diag_k, precision=highest)
        )
    diag_stack = jnp.stack(diag_terms, 0)
    halves = acc_columns.reshape(2, block, P_SIZE)
    mine = jnp.where(band_index == 0, halves[0], halves[1])
    theirs = jnp.where(band_index == 0, halves[1], halves[0])
    received = swapped(theirs, "tile", 1)
    grad_factor = lax.psum_scatter(mine + received, "cuts", scatter_dimension=0, tiled=True)
    padded = lax.dynamic_update_slice_in_dim(
        jnp.zeros((window_size, P_SIZE), F32), acc_window, band_index * rows_band, 0
    )
    window_part = lax.psum_scatter(padded, "cuts", scatter_dimension=0, tiled=True)
    window_total = lax.psum(window_part, "tile")
    core_total = lax.psum(acc_core, ("tile", "cuts"))
    diag_total = lax.psum(diag_stack, "tile")
    return (-coef * grad_factor, -coef * window_total, -coef * core_total, -coef * diag_total)


def body(trade, factor, scales, core):
    line = lax.axis_size("cuts") == 4 and lax.axis_size("tile") == 4
    if line and factor.shape[0] == 4 * trade.shape[2]:
        return body_line(trade, factor, scales, core)
    return body_any(trade, factor, scales, core)


def solution(mesh):
    return jax.shard_map(
        body,
        mesh=mesh,
        in_specs=(
            P(("groups", "cuts"), "tile", None, None),
            P(("groups", "tile", "cuts"), None),
            P(("groups", "cuts"), None),
            P("groups", None),
        ),
        out_specs=(
            P(("groups", "tile", "cuts"), None),
            P(("groups", "cuts"), None),
            P("groups", None),
            P(("groups", "cuts"), None),
        ),
        check_vma=False,
    )
```

```python
import functools
import math

import jax
import jax.numpy as jnp
from jax import lax
from jax.experimental import pallas as pl
from jax.experimental.pallas import tpu as pltpu
from jax.sharding import PartitionSpec as P

P_SIZE = 256
F32, BF16, F16 = jnp.float32, jnp.bfloat16, jnp.float16
NN = (((1,), (0,)), ((), ()))
NT = (((1,), (1,)), ((), ()))
TN = (((0,), (0,)), ((), ()))
VMEM_LIMIT = 48 * 2**20
VMEM_SMALL = 8 * 2**20
LARGE = pl.CostEstimate(flops=10**11, bytes_accessed=10**8, transcendentals=0)
SMALL = pl.CostEstimate(flops=1000, bytes_accessed=1000, transcendentals=0)


def dot(a, b, dims, **more):
    return lax.dot_general(a, b, dims, preferred_element_type=F32, **more)


def split3(value):
    first = value.astype(BF16)
    rest = value - first.astype(F32)
    second = rest.astype(BF16)
    return first, second, (rest - second.astype(F32)).astype(BF16)


def swapped(value, axis, mask):
    pairs = [(source, source ^ mask) for source in range(lax.axis_size(axis))]
    return lax.ppermute(value, axis, pairs)


def mapped_kernel(core_ref, window_ref, inner_ref, mapped_ref, turned_ref):
    rows = window_ref.shape[0] // 2
    at = core_ref[0]
    own = window_ref[pl.ds(pl.multiple_of(at * rows, rows), rows), :]
    other = window_ref[pl.ds(pl.multiple_of((1 - at) * rows, rows), rows), :]
    window = jnp.concatenate([own, other], 0)
    for month in range(inner_ref.shape[0]):
        value = sum(dot(window, term, NN) for term in split3(inner_ref[month]))
        rounded = value.astype(BF16)
        mapped_ref[month] = rounded
        turned_ref[:, month * 2 * rows : (month + 1) * 2 * rows] = rounded.astype(F32).T.astype(BF16)


def mapped_call(core_at, window, inner):
    months, size = inner.shape[0], window.shape[0]
    return pl.pallas_call(
        mapped_kernel,
        out_shape=[
            jax.ShapeDtypeStruct((months, size, P_SIZE), BF16),
            jax.ShapeDtypeStruct((P_SIZE, months * size), BF16),
        ],
        in_specs=[
            pl.BlockSpec(memory_space=pltpu.SMEM),
            pl.BlockSpec(memory_space=pltpu.VMEM),
            pl.BlockSpec(memory_space=pltpu.VMEM),
        ],
        out_specs=[pl.BlockSpec(memory_space=pltpu.VMEM)] * 2,
        compiler_params=pltpu.CompilerParams(vmem_limit_bytes=VMEM_SMALL),
        cost_estimate=SMALL,
        name="mapped",
    )(core_at, window, inner)


def half_kernel(at_ref, trade_ref, out_ref):
    out_ref[...] = trade_ref[:, 0]


def half_call(at, trade, half):
    months, rows = trade.shape[0], trade.shape[2]
    width = min(1024, half)
    steps = half // width
    return pl.pallas_call(
        half_kernel,
        grid_spec=pltpu.PrefetchScalarGridSpec(
            num_scalar_prefetch=1,
            grid=(steps,),
            in_specs=[pl.BlockSpec((months, 1, rows, width), lambda j, s: (0, 0, 0, s[0] * steps + j))],
            out_specs=pl.BlockSpec((months, rows, width), lambda j, s: (0, 0, j)),
        ),
        out_shape=jax.ShapeDtypeStruct((months, rows, half), trade.dtype),
        compiler_params=pltpu.CompilerParams(vmem_limit_bytes=VMEM_LIMIT),
        cost_estimate=LARGE,
        name="half",
    )(at, trade)


def encoded(value):
    peak = jnp.max(jnp.abs(value), axis=0, keepdims=True)
    exponent = jnp.ceil(jnp.log2(jnp.maximum(peak, 1e-30)))
    return value * jnp.exp2(15.0 - exponent), jnp.broadcast_to(exponent, (16, value.shape[1]))


def decoded(value):
    return value[:P_SIZE, :] * jnp.exp2(value[P_SIZE : P_SIZE + 1, :] - 15.0)


def piece_kernel(kind, chained, count, at_ref, own_ref, other_ref, *rest):
    blocks, (mapped_ref, turned_ref), rest = rest[:count], rest[count : count + 2], rest[count + 2 :]
    before_ref, outs = (rest[0], rest[1:]) if chained else (None, rest)
    grads, proj_ref = outs[:-1], outs[-1]
    step, width = pl.program_id(0), own_ref.shape[3]
    at = pl.multiple_of(step * width, width)
    if count == 1:
        block = blocks[0][pl.ds(at, width), :]
    else:
        block = jnp.where(step == 0, blocks[0][...], blocks[1][...])
    months, rows = mapped_ref.shape[0], mapped_ref.shape[1] // 2
    parts = []
    for month in range(months):
        for band in range(2):
            flows = own_ref[month, 0] if band == 0 else other_ref[month]
            model = dot(mapped_ref[month, band * rows : (band + 1) * rows, :], block, NT)
            parts.append((flows.astype(F32) - model).astype(BF16))
    residual = jnp.concatenate(parts, 0)
    grad = dot(turned_ref[...], residual, NN)
    if kind == "plain":
        grads[0][:, pl.ds(at, width)] = grad
    else:
        value, exponent = encoded(grad)
        grads[0][:P_SIZE, pl.ds(at, width)] = value
        grads[0][P_SIZE:, pl.ds(at, width)] = exponent
    projected = dot(residual, block, NN).reshape(proj_ref.shape)

    @pl.when(step == 0)
    def _():
        proj_ref[...] = before_ref[...] + projected if chained else projected

    @pl.when(step > 0)
    def _():
        proj_ref[...] += projected


def piece_call(at, trade, other, blocks, mapped, turned, before, kind, cost, label):
    months, size = mapped.shape[0], mapped.shape[1]
    rows, width = size // 2, sum(block.shape[0] for block in blocks) // 2
    vmem = pl.BlockSpec(memory_space=pltpu.VMEM)
    grads = {
        "plain": [(P_SIZE, 2 * width)],
        "coded": [(P_SIZE + 16, 2 * width)],
    }[kind]
    spec = pltpu.PrefetchScalarGridSpec(
        num_scalar_prefetch=1,
        grid=(2,),
        in_specs=[
            pl.BlockSpec((months, 1, rows, width), lambda j, s: (0, 0, 0, s[0] * 2 + j)),
            pl.BlockSpec((months, rows, width), lambda j, s: (0, 0, s[1] * 2 + j)),
        ]
        + [vmem] * (2 + len(blocks) + len(before)),
        out_specs=[vmem] * (len(grads) + 1),
    )
    return pl.pallas_call(
        functools.partial(piece_kernel, kind, len(before) > 0, len(blocks)),
        grid_spec=spec,
        out_shape=[jax.ShapeDtypeStruct(shape, F32) for shape in grads]
        + [jax.ShapeDtypeStruct((months, size, P_SIZE), F32)],
        compiler_params=pltpu.CompilerParams(vmem_limit_bytes=VMEM_LIMIT),
        cost_estimate=cost,
        name=label,
    )(at, trade, other, *blocks, mapped, turned, *before)


def relay_kernel(received_ref, own_ref, *outs):
    step = pl.program_id(0)
    value, exponent = encoded(decoded(received_ref[...]) + own_ref[...])
    for index, ref in enumerate(outs):

        @pl.when(step == index)
        def _():
            ref[:P_SIZE, :] = value
            ref[P_SIZE:, :] = exponent


def relay_call(received, own):
    width = own.shape[1] // 2
    vmem = pl.BlockSpec(memory_space=pltpu.VMEM)
    return pl.pallas_call(
        relay_kernel,
        grid=(2,),
        in_specs=[
            pl.BlockSpec((P_SIZE + 16, width), lambda j: (0, j)),
            pl.BlockSpec((P_SIZE, width), lambda j: (0, j)),
        ],
        out_specs=[vmem, vmem],
        out_shape=[jax.ShapeDtypeStruct((P_SIZE + 16, width), F32)] * 2,
        compiler_params=pltpu.CompilerParams(vmem_limit_bytes=VMEM_SMALL),
        cost_estimate=SMALL,
        name="relay",
    )(received, own)


def final_kernel(coef, own_ref, near_ref, first_ref, second_ref, out_ref):
    far = jnp.where(pl.program_id(0) == 0, first_ref[...], second_ref[...])
    total = own_ref[...] + decoded(near_ref[...]) + decoded(far)
    out_ref[...] = (-coef * total).T


def final_call(coef, own, near, halves):
    columns = own.shape[1]
    width = columns // 2
    vmem = pl.BlockSpec(memory_space=pltpu.VMEM)
    return pl.pallas_call(
        functools.partial(final_kernel, coef),
        grid=(2,),
        in_specs=[
            pl.BlockSpec((P_SIZE, width), lambda j: (0, j)),
            pl.BlockSpec((P_SIZE + 16, width), lambda j: (0, j)),
            vmem,
            vmem,
        ],
        out_specs=pl.BlockSpec((width, P_SIZE), lambda j: (j, 0)),
        out_shape=jax.ShapeDtypeStruct((columns, P_SIZE), F32),
        compiler_params=pltpu.CompilerParams(vmem_limit_bytes=VMEM_SMALL),
        cost_estimate=SMALL,
        name="final",
    )(own, near, *halves)


def terms_kernel(cuts, at_ref, window_ref, inner_ref, core_ref, scales_ref, columns_ref, *rest):
    projs, outs, acc_ref = rest[:-5], rest[-5:-1], rest[-1]
    months, size = projs[0].shape[0], projs[0].shape[1]
    rows = size // 2
    tile, cut = at_ref[0], at_ref[1]
    at = tile % 2
    own = window_ref[pl.ds(pl.multiple_of(at * rows, rows), rows), :]
    other = window_ref[pl.ds(pl.multiple_of((1 - at) * rows, rows), rows), :]
    window = jnp.concatenate([own, other], 0)
    core = core_ref[...]
    acc_window = jnp.zeros((size, P_SIZE), F32)
    acc_core = jnp.zeros((P_SIZE, P_SIZE), F32)
    diagonals = []
    for month in range(months):
        proj = projs[0][month]
        for ref in projs[1:]:
            proj = proj + ref[month]
        acc_window = acc_window + dot(proj, inner_ref[month], NT, precision=lax.Precision.HIGHEST)
        gram = sum(dot(window, term, TN) for term in split3(proj))
        down = columns_ref[:, month : month + 1]
        acc_core = acc_core + down * gram * scales_ref[month : month + 1, :]
        weighted = gram * core
        diagonals.append(jnp.sum((weighted + weighted.T) * down, axis=0, keepdims=True))
    diagonals.append(jnp.zeros((8 - months, P_SIZE), F32))
    diagonal = jnp.concatenate(diagonals, 0)
    acc_ref[pl.ds(pl.multiple_of(at * rows, rows), rows), :] = acc_window[:rows]
    acc_ref[pl.ds(pl.multiple_of((1 - at) * rows, rows), rows), :] = acc_window[rows:]
    acc_ref[size:, :] = acc_core
    w, q = size // (4 * cuts), P_SIZE // 4
    for mask, ref in enumerate(outs):
        for turn in range(cuts):
            start = pl.multiple_of((cut ^ turn) * 4 * w + (tile ^ mask) * w, 8)
            ref[turn * w : (turn + 1) * w, :] = acc_ref[pl.ds(start, w), :]
        start = pl.multiple_of(size + (tile ^ mask) * q, 8)
        ref[cuts * w : cuts * w + q, :] = acc_ref[pl.ds(start, q), :]
        ref[cuts * w + q :, :] = diagonal


def terms_call(cuts, place, window, inner, core, scales, projs):
    months, size = projs[0].shape[0], projs[0].shape[1]
    high = size // 4 + P_SIZE // 4 + 8
    vmem = pl.BlockSpec(memory_space=pltpu.VMEM)
    return pl.pallas_call(
        functools.partial(terms_kernel, cuts),
        in_specs=[pl.BlockSpec(memory_space=pltpu.SMEM)] + [vmem] * (5 + len(projs)),
        out_specs=[vmem] * 4,
        out_shape=[jax.ShapeDtypeStruct((high, P_SIZE), F32)] * 4,
        scratch_shapes=[pltpu.VMEM((size + P_SIZE, P_SIZE), F32)],
        compiler_params=pltpu.CompilerParams(vmem_limit_bytes=VMEM_SMALL),
        cost_estimate=SMALL,
        name="terms",
    )(place, window, inner, core, scales, scales.T, *projs)


def quarter_kernel(cuts, own_ref, *rest):
    received, outs, diagonal_ref = rest[:3], rest[3:-1], rest[-1]
    total = own_ref[...]
    for ref in received:
        total = total + ref[...]
    w, q = (total.shape[0] - 8 - P_SIZE // 4) // cuts, P_SIZE // 4
    for turn, ref in enumerate(outs):
        ref[:w, :] = total[turn * w : (turn + 1) * w, :]
        ref[w:, :] = total[cuts * w : cuts * w + q, :]
    diagonal_ref[...] = total[cuts * w + q :, :]


def quarter_call(cuts, own, received):
    w, q = (own.shape[0] - 8 - P_SIZE // 4) // cuts, P_SIZE // 4
    vmem = pl.BlockSpec(memory_space=pltpu.VMEM)
    return pl.pallas_call(
        functools.partial(quarter_kernel, cuts),
        in_specs=[vmem] * 4,
        out_specs=[vmem] * (cuts + 1),
        out_shape=[jax.ShapeDtypeStruct((w + q, P_SIZE), F32)] * cuts
        + [jax.ShapeDtypeStruct((8, P_SIZE), F32)],
        compiler_params=pltpu.CompilerParams(vmem_limit_bytes=VMEM_SMALL),
        cost_estimate=SMALL,
        name="quarter",
    )(own, *received)


def join_kernel(coef, at_ref, *rest):
    parts, diagonal_ref, (window_ref, core_ref, scales_ref) = rest[:4], rest[4], rest[5:]
    tile = at_ref[0]
    w, q = window_ref.shape[0] // 4, core_ref.shape[0] // 4
    for mask, ref in enumerate(parts):
        window_ref[pl.ds(pl.multiple_of((tile ^ mask) * w, 8), w), :] = -coef * ref[:w, :]
        core_ref[pl.ds(pl.multiple_of((tile ^ mask) * q, 8), q), :] = -coef * ref[w:, :]
    scales_ref[...] = -coef * diagonal_ref[: scales_ref.shape[0], :]


def join_call(coef, months, place, parts, diagonal):
    q = P_SIZE // 4
    w = parts[0].shape[0] - q
    vmem = pl.BlockSpec(memory_space=pltpu.VMEM)
    return pl.pallas_call(
        functools.partial(join_kernel, coef),
        in_specs=[pl.BlockSpec(memory_space=pltpu.SMEM)] + [vmem] * 5,
        out_specs=[vmem] * 3,
        out_shape=[jax.ShapeDtypeStruct((high, P_SIZE), F32) for high in (4 * w, P_SIZE, months)],
        compiler_params=pltpu.CompilerParams(vmem_limit_bytes=VMEM_SMALL),
        cost_estimate=SMALL,
        name="join",
    )(place, *parts, diagonal)


def body_line(trade, factor, scales, core):
    cuts = lax.axis_size("cuts")
    tile, cut = lax.axis_index("tile"), lax.axis_index("cuts")
    at = tile % 2
    months, rows = trade.shape[0], trade.shape[2]
    size, piece = 2 * rows, factor.shape[0]
    coef = 1.0 / math.sqrt(months * cuts * size)
    place = jnp.stack([tile, cut]).astype(jnp.int32)
    core_at = at.astype(jnp.int32).reshape(1)
    inner = scales[:, :, None] * core[None] * scales[:, None, :]
    hold = lax.optimization_barrier

    half = cuts * piece
    give = half_call((1 - at).astype(jnp.int32).reshape(1), trade, half)

    parts = [factor[:size], factor[size:]]
    second = lax.ppermute(parts[0], ("tile", "cuts"), [(0, 2)])
    far = [swapped(value, "cuts", 3) for value in parts]
    near = [swapped(value, "cuts", 1) for value in parts]
    second, near[0], far[0], give = hold((second, near[0], far[0], give))
    other = swapped(give, "tile", 1)
    line = jnp.where(cut == 0, parts[0], jnp.where(cut == 1, near[0], jnp.where(cut == 2, second, far[0])))
    out = [lax.ppermute(line, "tile", [(0, target)]) for target in (3, 2, 1)]
    window = jnp.where(tile == 0, line, sum(out[1:], out[0]))
    mapped, turned = mapped_call(core_at, window, inner)

    def piece_of(which, blocks, kind, cost, label, before, after=None):
        where = jnp.stack([at * cuts + which, which]).astype(jnp.int32)
        if after is not None:
            where, _ = hold((where, after))
        return piece_call(where, trade, other, blocks, mapped, turned, before, kind, cost, label)

    grad_own, proj = piece_of(cut, [factor], "plain", LARGE, "piece_own", [])
    far[1], _ = hold((far[1], proj))
    middle = [swapped(value, "cuts", 1) for value in far]
    grad_far, proj = piece_of(cut ^ 3, far, "coded", SMALL, "piece_far", [proj], proj)
    grad_far = grad_far.astype(F16)
    joined = swapped(grad_far, "cuts", 1)
    grad_near, proj = piece_of(cut ^ 1, near, "coded", LARGE, "piece_near", [proj], grad_far)
    grad_near = grad_near.astype(F16)
    from_near = swapped(grad_near, "cuts", 1)
    grad_middle, proj = piece_of(cut ^ 2, middle, "plain", LARGE, "piece_middle", [proj], grad_near)

    own, *send = terms_call(cuts, place, window, inner, core, scales, [proj])
    received = [swapped(send[mask - 1], "tile", mask) for mask in (3, 2, 1)][::-1]
    joined, received[0] = hold((joined, received[0]))
    passed = list(relay_call(joined.astype(F32), grad_middle))
    from_middle = swapped(passed[0].astype(F16), "cuts", 2)
    own, *send, diagonal = quarter_call(cuts, own, received)
    send, passed[1] = hold((send, passed[1]))
    from_middle_second = swapped(passed[1].astype(F16), "cuts", 2)
    send = [swapped(value, "cuts", mask + 1) for mask, value in enumerate(send)]
    send, from_near, from_middle = hold((send, from_near, from_middle))
    total = own + sum(send)
    quarters = [swapped(total, "tile", mask) for mask in (3, 2, 1)][::-1]
    halves = [from_middle.astype(F32), from_middle_second.astype(F32)]
    grad_factor = final_call(coef, grad_own, from_near.astype(F32), halves)
    quarters, grad_factor = hold((quarters, grad_factor))
    grad_window, grad_core, grad_scales = join_call(coef, months, place, [total] + quarters, diagonal)
    return (grad_factor, grad_window, grad_core, grad_scales)


def from_root(block, axis, source):
    block = jnp.where(lax.axis_index(axis) == source, block, jnp.zeros_like(block))
    return lax.psum(block, axis)


def body_any(trade, factor, scales, core):
    n_cuts = lax.axis_size("cuts")
    band_index = lax.axis_index("tile") % 2
    months = trade.shape[0]
    rows_band = trade.shape[2]
    window_size = 2 * rows_band
    highest = lax.Precision.HIGHEST
    own_block = lax.all_gather(factor, "cuts", axis=0, tiled=True)
    block = own_block.shape[0]
    partner_block = swapped(own_block, "tile", 1)
    first_block = jnp.where(band_index == 0, own_block, partner_block)
    second_block = jnp.where(band_index == 0, partner_block, own_block)
    column_factor = jnp.concatenate([first_block, second_block], 0)
    window_block = from_root(own_block, "tile", 0)
    window_rows = lax.dynamic_slice_in_dim(window_block, band_index * rows_band, rows_band, 0)
    window32 = window_rows.astype(F32)
    coef = 1.0 / math.sqrt(months * n_cuts * window_size)
    acc_columns = jnp.zeros((2 * block, P_SIZE), F32)
    acc_window = jnp.zeros((rows_band, P_SIZE), F32)
    acc_core = jnp.zeros((P_SIZE, P_SIZE), F32)
    diag_terms = []
    for month in range(months):
        diag_k = scales[month]
        inner = diag_k[:, None] * core * diag_k[None, :]
        mapped = jnp.dot(window32, inner, precision=highest).astype(BF16)
        model = dot(mapped, column_factor, NT)
        residual = (trade[month, 0].astype(F32) - model).astype(BF16)
        acc_columns = acc_columns + dot(residual, mapped, TN)
        projected = dot(residual, column_factor, NN)
        acc_window = acc_window + jnp.dot(projected, inner.T, precision=highest)
        gram = jnp.dot(window32.T, projected, precision=highest)
        acc_core = acc_core + diag_k[:, None] * gram * diag_k[None, :]
        weighted = gram * core
        diag_terms.append(
            jnp.dot(weighted, diag_k, precision=highest) + jnp.dot(weighted.T, diag_k, precision=highest)
        )
    diag_stack = jnp.stack(diag_terms, 0)
    halves = acc_columns.reshape(2, block, P_SIZE)
    mine = jnp.where(band_index == 0, halves[0], halves[1])
    theirs = jnp.where(band_index == 0, halves[1], halves[0])
    received = swapped(theirs, "tile", 1)
    grad_factor = lax.psum_scatter(mine + received, "cuts", scatter_dimension=0, tiled=True)
    padded = lax.dynamic_update_slice_in_dim(
        jnp.zeros((window_size, P_SIZE), F32), acc_window, band_index * rows_band, 0
    )
    window_part = lax.psum_scatter(padded, "cuts", scatter_dimension=0, tiled=True)
    window_total = lax.psum(window_part, "tile")
    core_total = lax.psum(acc_core, ("tile", "cuts"))
    diag_total = lax.psum(diag_stack, "tile")
    return (-coef * grad_factor, -coef * window_total, -coef * core_total, -coef * diag_total)


def body(trade, factor, scales, core):
    line = lax.axis_size("cuts") == 4 and lax.axis_size("tile") == 4
    if line and factor.shape[0] == 4 * trade.shape[2]:
        return body_line(trade, factor, scales, core)
    return body_any(trade, factor, scales, core)


def solution(mesh):
    return jax.shard_map(
        body,
        mesh=mesh,
        in_specs=(
            P(("groups", "cuts"), "tile", None, None),
            P(("groups", "tile", "cuts"), None),
            P(("groups", "cuts"), None),
            P("groups", None),
        ),
        out_specs=(
            P(("groups", "tile", "cuts"), None),
            P(("groups", "cuts"), None),
            P("groups", None),
            P(("groups", "cuts"), None),
        ),
        check_vma=False,
    )
```
